128 devices in a mesh: dp: 8 (over x_lo, y), seq: 16 (over z, x_hi, core).
Axes of the slice: x: 4 (x_hi: 2, x_lo: 2; x = x_hi * 2 + x_lo), y: 4, z: 4, core: 2. Of those that a mesh axis runs over, the one named last changes fastest.
Arguments:
- queries: bfloat16 [16384, 1152], P(('dp', 'seq')), may hold values from -6 to 6
- keys: bfloat16 [16384, 1152], P(('dp', 'seq')), may hold values from -6 to 6
- values: bfloat16 [16384, 1152], P(('dp', 'seq')), may hold values from -6 to 6
- out_grad: bfloat16 [16384, 1152], P(('dp', 'seq')), may hold values from -24 to 24
- out_weight: bfloat16 [1152, 1152], replicated, may hold values from -0.1875 to 0.1875
- extents: int32 [8, 8], P('dp'), may hold values from 1 to 16, 32 in all within a row
Outputs:
- query_grad: bfloat16 [16384, 1152], P(('dp', 'seq'))
- key_grad: bfloat16 [16384, 1152], P(('dp', 'seq'))
- value_grad: bfloat16 [16384, 1152], P(('dp', 'seq'))
- weight_grad: float32 [1152, 1152], P('seq', 'dp')
The draws below stay inside these ranges and needn't reach their ends.
Inputs may be any that keep to these rules, and one draw needn't show every extreme that they name: `extents`: row i lists the 8 images packed in order into sequence i, in units of 64 tokens; each row sums to 32.
All inputs are finite; a program needn't handle non-finite values.
Results may differ from the reference program's by a relative error of at most 0.034.
Values may be sent and summed in bfloat16 or wider, within the bound.
No kernel may reach another device: no remote copies, remote signals or barrier semaphores. Data moves between devices by JAX's collectives and lax.ppermute only.
A program may use at most 128 MiB of HBM per device.

```python
import math
import jax
import jax.numpy as jnp
import numpy as np
from jax import lax

D = 1152
HEADS = 16
HEAD = 72
IMAGES = 8
UNIT = 64
SEQ = 2048
TOKENS = 16384
SEQ_UNITS = 32
MOST_UNITS = 16
N_DP = 8


def draw_queries(key, part):
    key = jax.random.fold_in(key, 11)
    result = jnp.clip(jax.random.normal(key, (TOKENS, D), jnp.float32), -4.0, 4.0)
    return result.astype(jnp.bfloat16)


def draw_keys(key, part):
    key = jax.random.fold_in(key, 23)
    result = jnp.clip(jax.random.normal(key, (TOKENS, D), jnp.float32), -4.0, 4.0)
    return result.astype(jnp.bfloat16)


def strengthened(drawn, stream_key, source, target, parts, factor):
    def block_of(axis_at):
        return (jnp.arange(drawn.shape[axis_at]) // (drawn.shape[axis_at] // parts)).reshape((-1,) + (1,) * (drawn.ndim - 1 - axis_at))

    one_side = jax.random.permutation(stream_key, parts)[block_of(target)]
    other_side = (block_of(target) + parts // 2) % parts
    return jnp.where((block_of(source) == one_side) | (block_of(source) == other_side), factor * drawn, drawn)


def steps_of(stream_key, dims, pieces, smallest, top_value):
    def one(dim, parts):
        heights = jax.random.uniform(jax.random.fold_in(jax.random.fold_in(stream_key, 6), dim), (parts,), jnp.float32, smallest / len(pieces), top_value / len(pieces))
        return jnp.repeat(jnp.exp(heights), dims[dim] // parts).reshape((-1,) + (1,) * (len(dims) - dim - 1))

    loudness = one(*pieces[0])
    for cut in pieces[1:]:
        loudness = loudness * one(*cut)
    return loudness


def length_profile(count, total, most, lean):
    loads = [(1 << 20) // math.isqrt(grade ** lean) + 1 for grade in range(2, count + 1)]
    rest, counts = total - most - (count - 1), [1] * (count - 1)
    while rest > 0:
        movable = [i for i in range(count - 1) if counts[i] < most]
        mass, budget = sum([loads[i] for i in movable]), rest
        for i in movable:
            extra = min(most - counts[i], max(1, budget * loads[i] // mass), rest)
            counts[i] = counts[i] + extra
            rest = rest - extra
    return np.array([most] + counts)


def uneven_parts(own_key, amount, total, limit, slope):
    if amount == 2:
        one = jax.random.randint(own_key, (), max(1, total - limit), min(limit, total - 1) + 1)
        return jnp.stack([one, total - one])
    sizes = jnp.asarray(length_profile(amount, total, limit, slope), jnp.int32)
    couples = (amount - 1) // 2
    source_of, receiver = sizes[1:1 + 2 * couples:2], sizes[2:2 + 2 * couples:2]
    slack = jnp.minimum(source_of - 1, limit - receiver)
    passed = jax.random.randint(jax.random.fold_in(own_key, 1), (couples,), 0, 1 << 20) % (slack + 1)
    sizes = sizes.at[1:1 + 2 * couples:2].set(source_of - passed).at[2:2 + 2 * couples:2].set(receiver + passed)
    return sizes[jax.random.permutation(jax.random.fold_in(own_key, 2), amount)]


def scatter_about(rng, extent, scale, bound, pieces=(), kind=jnp.bfloat16):
    factor_of = steps_of(rng, extent, pieces, -0.22, 0.18) if pieces else 1.0
    drawn = jax.random.normal(rng, extent, jnp.float32) * scale * factor_of
    return jnp.minimum(jnp.maximum(drawn, -bound), bound).astype(kind)


def bell_draw_with(stream_key, extent, spread, reach, shards, heavy, kind=jnp.bfloat16):
    array = spread * jax.random.normal(stream_key, extent, jnp.float32)
    if shards:
        array = array * steps_of(stream_key, extent, shards, -0.22, 0.18)
    return jnp.clip(strengthened(array, jax.random.fold_in(stream_key, 3), *heavy), -reach, reach).astype(kind)


def setup_inputs(seed: int = 0) -> dict:
    key_of = jax.random.split(jax.random.key(seed), 7)
    queries = draw_queries(jax.random.fold_in(key_of[6], 71), 0)
    keys = draw_keys(jax.random.fold_in(key_of[6], 71), 0)
    values = scatter_about(key_of[2], (TOKENS, D), 1.0, 6.0, ((0, 128),))
    out_grad = bell_draw_with(key_of[3], (TOKENS, D), 1.0, 24.0, ((0, 128),), (0, 1, 128, 5.5))
    out_weight = scatter_about(key_of[4], (D, D), D ** -0.5, 0.1875)
    extents = jax.vmap(lambda own: uneven_parts(own, IMAGES, SEQ_UNITS, MOST_UNITS, 2))(jax.random.split(key_of[5], N_DP)).reshape((N_DP, IMAGES)).astype(jnp.int32)
    return dict(queries=queries, keys=keys, values=values, out_grad=out_grad, out_weight=out_weight, extents=extents)


def attend_head(query_head, key_head, value_head, back_head, same):
    score_scale = HEAD ** -0.5
    scores = jnp.dot(query_head, key_head.T, preferred_element_type=jnp.float32) * score_scale
    masked = jnp.where(same, scores, -1e30)
    top_score = jnp.max(masked, axis=1, keepdims=True)
    total = jnp.sum(jnp.where(same, jnp.exp(scores - top_score), 0.0), axis=1, keepdims=True)
    log_total = top_score + jnp.log(total)
    probs = jnp.where(same, jnp.exp(scores - log_total), 0.0)
    probs_low = probs.astype(jnp.bfloat16)
    attended = jnp.dot(probs_low, value_head, preferred_element_type=jnp.float32).astype(jnp.bfloat16)
    delta = jnp.sum(back_head.astype(jnp.float32) * attended.astype(jnp.float32), axis=1, keepdims=True)
    dprobs = jnp.dot(back_head, value_head.T, preferred_element_type=jnp.float32)
    dscores = (probs * (dprobs - delta)).astype(jnp.bfloat16)
    query_grad = (jnp.dot(dscores, key_head, preferred_element_type=jnp.float32) * score_scale).astype(jnp.bfloat16)
    key_grad = (jnp.dot(dscores.T, query_head, preferred_element_type=jnp.float32) * score_scale).astype(jnp.bfloat16)
    value_grad = jnp.dot(probs_low.T, back_head, preferred_element_type=jnp.float32).astype(jnp.bfloat16)
    return attended, query_grad, key_grad, value_grad


def split_heads(matrix):
    return matrix.reshape(SEQ, HEADS, HEAD).transpose(1, 0, 2)


def merge_heads(stacked):
    return stacked.transpose(1, 0, 2).reshape(SEQ, D)


def sequence_grads(inputs, out_weight):
    queries, keys, values, out_grad, extent_row = inputs
    image_ends = jnp.cumsum(extent_row).astype(jnp.int32) * UNIT
    position = jnp.arange(SEQ, dtype=jnp.int32)
    segment = jnp.sum((position[:, None] >= image_ends[None, :]).astype(jnp.int32), axis=1)
    same = segment[:, None] == segment[None, :]
    out_back = jnp.dot(out_grad, out_weight.T, preferred_element_type=jnp.float32).astype(jnp.bfloat16)

    def one_head(head_inputs):
        return attend_head(head_inputs[0], head_inputs[1], head_inputs[2], head_inputs[3], same)

    attended, query_grad, key_grad, value_grad = lax.map(
        one_head, (split_heads(queries), split_heads(keys), split_heads(values), split_heads(out_back)))
    return merge_heads(attended), merge_heads(query_grad), merge_heads(key_grad), merge_heads(value_grad)


def reference(queries, keys, values, out_grad, out_weight, extents):
    def per_sequence(inputs):
        return sequence_grads(inputs, out_weight)

    stacked = (queries.reshape(N_DP, SEQ, D), keys.reshape(N_DP, SEQ, D), values.reshape(N_DP, SEQ, D),
               out_grad.reshape(N_DP, SEQ, D), extents)
    attended, query_grad, key_grad, value_grad = lax.map(per_sequence, stacked)
    attended = attended.reshape(TOKENS, D)
    weight_grad = jnp.dot(attended.T, out_grad, preferred_element_type=jnp.float32)
    return (query_grad.reshape(TOKENS, D), key_grad.reshape(TOKENS, D), value_grad.reshape(TOKENS, D), weight_grad)
```

```python
import functools

import jax
import jax.numpy as jnp
from jax import lax
from jax.experimental import pallas as pl
from jax.experimental.pallas import tpu as pltpu
from jax.sharding import PartitionSpec as P

HEADS = 16
HEAD = 72
IMAGES = 8
UNIT = 64
ROWS = 128
BLOCK = 256
BLOCKS = 8
PAD = 80
SCALE = HEAD**-0.5
LOG2E = 1.4426950408889634
FAR = 16384.0
F32 = jnp.float32
BF16 = jnp.bfloat16
VMEM_LIMIT = 48 * 1024 * 1024

NN = (((1,), (0,)), ((), ()))
NT = (((1,), (1,)), ((), ()))


def dot(a, b, dims):
    return lax.dot_general(a, b, dims, preferred_element_type=F32)


def pack_body(q_ref, k_ref, v_ref, g_ref, w_ref, out_ref):
    back = dot(w_ref[...], g_ref[...], NT).astype(BF16).astype(F32)
    parts = [ref[...].astype(F32).T for ref in (q_ref, k_ref, v_ref)] + [back]
    for h in range(HEADS):
        rows = slice(h * HEAD, (h + 1) * HEAD)
        out_ref[h] = jnp.concatenate([part[rows] for part in parts], axis=0).astype(BF16)


def pack(queries, keys, values, out_grad, out_weight):
    return pl.pallas_call(
        pack_body,
        out_shape=jax.ShapeDtypeStruct((HEADS, 4 * HEAD, ROWS), BF16),
        compiler_params=pltpu.CompilerParams(vmem_limit_bytes=VMEM_LIMIT),
        name="pack",
    )(queries, keys, values, out_grad, out_weight)


def attend_body(
    ext_ref, r_ref, g_ref, att_ref, q_s, b_s, k_s, v_s, kn_s, vn_s, e_s, dq_s, dk_s, dv_s
):
    ends = []
    total = jnp.int32(0)
    for i in range(IMAGES):
        total = total + ext_ref[0, i] * UNIT
        ends.append(total)

    lane = lax.broadcasted_iota(jnp.int32, (IMAGES, ROWS), 1)
    row = lax.broadcasted_iota(jnp.int32, (IMAGES, ROWS), 0)
    nothing = jnp.zeros((128 - PAD, ROWS), F32)
    ones_row = jnp.where(row == 0, 1.0, 0.0)
    zeros_rows = jnp.zeros((IMAGES, ROWS), F32)
    for s in range(HEADS):
        b, half = s // 2, s % 2
        lanes = slice(half * ROWS, (half + 1) * ROWS)
        x = r_ref[s].astype(F32)
        q, k, v, back = (x[j * HEAD : (j + 1) * HEAD] for j in range(4))
        segment = jnp.zeros((IMAGES, ROWS), jnp.int32)
        for end in ends:
            segment = segment + (lane + s * ROWS >= end).astype(jnp.int32)
        here = (segment == row).astype(F32)
        q_s[b, :, lanes] = jnp.concatenate([q, here * -FAR, nothing], axis=0).astype(BF16)
        b_s[b, :, lanes] = jnp.concatenate([back, zeros_rows], axis=0).astype(BF16)
        k_aug = jnp.concatenate([k, 1.0 - here, nothing], axis=0)
        v_aug = jnp.concatenate([v, zeros_rows, nothing], axis=0)
        k_s[b, :, lanes] = k_aug[:PAD].astype(BF16)
        v_s[b, :, lanes] = jnp.concatenate([v, ones_row], axis=0).astype(BF16)
        kn_s[b, lanes, :] = k_aug.T.astype(BF16)
        vn_s[b, lanes, :] = v_aug.T.astype(BF16)

    dk_s[...] = jnp.zeros_like(dk_s)
    dv_s[...] = jnp.zeros_like(dv_s)

    def query_block(qb, carry):
        first = qb * BLOCK
        last = first + BLOCK - 1
        start, stop = jnp.int32(0), jnp.int32(BLOCKS * BLOCK)
        for end in ends:
            start = jnp.maximum(start, jnp.where(end <= first, end, 0))
            stop = jnp.minimum(stop, jnp.where(end > last, end, BLOCKS * BLOCK))
        lo = start // BLOCK
        hi = (stop + BLOCK - 1) // BLOCK
        q = q_s[qb]

        def scores_of(c, top):
            scores = dot(kn_s[c], q, NN)
            e_s[c] = scores
            return jnp.maximum(top, jnp.max(scores.reshape(BLOCK // 8, 8, BLOCK), axis=0))

        top = lax.fori_loop(lo, hi, scores_of, jnp.full((8, BLOCK), -3e38, F32))
        top = jnp.max(top, axis=0, keepdims=True)

        def attend(c, acc):
            e = jnp.exp2((e_s[c] - top) * (SCALE * LOG2E))
            e_s[c] = e
            return acc + dot(v_s[c], e.astype(BF16), NN)

        acc = lax.fori_loop(lo, hi, attend, jnp.zeros((PAD, BLOCK), F32))
        inverse = 1.0 / acc[HEAD : HEAD + 1]
        attended = (acc[:HEAD] * inverse).astype(BF16)
        att_ref[2 * qb] = attended[:, :ROWS]
        att_ref[2 * qb + 1] = attended[:, ROWS:]
        back = b_s[qb].astype(F32)
        delta = jnp.sum(back[:HEAD] * attended.astype(F32), axis=0, keepdims=True) * inverse
        back = (back * inverse).astype(BF16)
        back_wide = jnp.concatenate([back, jnp.zeros((128 - PAD, BLOCK), BF16)], axis=0)

        def grads(c, dq):
            e = e_s[c]
            ds = (e * (dot(vn_s[c], back_wide, NN) - delta)).astype(BF16)
            dv_s[c] += dot(back, e.astype(BF16), NT)
            dk_s[c] += dot(q[:PAD], ds, NT)
            return dq + dot(k_s[c], ds, NN)

        dq_s[qb] = lax.fori_loop(lo, hi, grads, jnp.zeros((PAD, BLOCK), F32))
        return carry

    lax.fori_loop(0, BLOCKS, query_block, 0)

    for s in range(HEADS):
        b, half = s // 2, s % 2
        lanes = slice(half * ROWS, (half + 1) * ROWS)
        g_ref[s] = jnp.concatenate(
            [
                dq_s[b, :HEAD, lanes] * SCALE,
                dk_s[b, :HEAD, lanes] * SCALE,
                dv_s[b, :HEAD, lanes],
            ],
            axis=0,
        ).astype(BF16)


def attend(extents, received):
    return pl.pallas_call(
        attend_body,
        out_shape=(
            jax.ShapeDtypeStruct((HEADS, 3 * HEAD, ROWS), BF16),
            jax.ShapeDtypeStruct((HEADS, HEAD, ROWS), BF16),
        ),
        in_specs=[
            pl.BlockSpec(memory_space=pltpu.SMEM),
            pl.BlockSpec(memory_space=pltpu.VMEM),
        ],
        scratch_shapes=[
            pltpu.VMEM((BLOCKS, 128, BLOCK), BF16),
            pltpu.VMEM((BLOCKS, PAD, BLOCK), BF16),
            pltpu.VMEM((BLOCKS, PAD, BLOCK), BF16),
            pltpu.VMEM((BLOCKS, PAD, BLOCK), BF16),
            pltpu.VMEM((BLOCKS, BLOCK, 128), BF16),
            pltpu.VMEM((BLOCKS, BLOCK, 128), BF16),
            pltpu.VMEM((BLOCKS, BLOCK, BLOCK), F32),
            pltpu.VMEM((BLOCKS, PAD, BLOCK), F32),
            pltpu.VMEM((BLOCKS, PAD, BLOCK), F32),
            pltpu.VMEM((BLOCKS, PAD, BLOCK), F32),
        ],
        compiler_params=pltpu.CompilerParams(vmem_limit_bytes=VMEM_LIMIT),
        name="attend",
    )(extents, received)


def unpack_body(y_ref, dq_ref, dk_ref, dv_ref):
    for j, ref in enumerate((dq_ref, dk_ref, dv_ref)):
        rows = [y_ref[h].astype(F32)[j * HEAD : (j + 1) * HEAD] for h in range(HEADS)]
        ref[...] = jnp.concatenate(rows, axis=0).T.astype(BF16)


def unpack(returned):
    shape = jax.ShapeDtypeStruct((ROWS, HEADS * HEAD), BF16)
    return pl.pallas_call(
        unpack_body,
        out_shape=(shape, shape, shape),
        compiler_params=pltpu.CompilerParams(vmem_limit_bytes=VMEM_LIMIT),
        name="unpack",
    )(returned)


def local(queries, keys, values, out_grad, out_weight, extents):
    same_core = [[core + 2 * chip for chip in range(8)] for core in range(2)]
    swap_core = [(i, i ^ 1) for i in range(HEADS)]
    core = lax.axis_index("seq") % 2

    sent = pack(queries, keys, values, out_grad, out_weight)
    received = lax.all_to_all(sent, "seq", 0, 0, tiled=True)
    copies = jnp.broadcast_to(out_grad[None], (8,) + out_grad.shape)
    grad_all = lax.all_to_all(copies, "seq", 0, 0, tiled=True, axis_index_groups=same_core)
    grads, attended = attend(extents, received)
    returned = lax.all_to_all(grads, "seq", 0, 0, tiled=True)
    query_grad, key_grad, value_grad = unpack(returned)

    by_core = attended.reshape(8, 2, HEAD, ROWS)
    mine = lax.dynamic_index_in_dim(by_core, core, 1, keepdims=False)
    other = lax.dynamic_index_in_dim(by_core, 1 - core, 1, keepdims=False)
    other = lax.ppermute(other, "seq", swap_core)

    def term(rows):
        return jnp.einsum("shr,srd->hd", rows, grad_all, preferred_element_type=F32)

    passed = lax.ppermute(term(other).astype(BF16), "seq", swap_core)
    summed = (term(mine) + passed.astype(F32)).astype(BF16)
    tiles = summed.reshape(HEAD, 8, 144).transpose(1, 0, 2)
    tiles = lax.all_to_all(tiles, "dp", 0, 0, tiled=True)
    weight_grad = jnp.sum(tiles.astype(F32), axis=0)
    return query_grad, key_grad, value_grad, weight_grad


def solution(mesh):
    tokens = P(("dp", "seq"), None)
    return jax.shard_map(
        local,
        mesh=mesh,
        in_specs=(tokens, tokens, tokens, tokens, P(), P("dp", None)),
        out_specs=(tokens, tokens, tokens, P("seq", "dp")),
        check_vma=False,
    )
```

```python
import functools

import jax
import jax.numpy as jnp
from jax import lax
from jax.experimental import pallas as pl
from jax.experimental.pallas import tpu as pltpu
from jax.sharding import PartitionSpec as P

HEADS = 16
HEAD = 72
IMAGES = 8
UNIT = 64
ROWS = 128
BLOCK = 256
BLOCKS = 8
PAIRS = BLOCKS * BLOCKS + 8
PAD = 80
SCALE = HEAD**-0.5
LOG2E = 1.4426950408889634
FAR = 16384.0
F32 = jnp.float32
BF16 = jnp.bfloat16
VMEM_LIMIT = 48 << 20
VMEM_MOST = (64 << 20) - (128 << 10)

NN = (((1,), (0,)), ((), ()))
NT = (((1,), (1,)), ((), ()))


def dot(a, b, dims):
    return lax.dot_general(a, b, dims, preferred_element_type=F32)


def pack_body(q_hbm, k_hbm, v_hbm, g_hbm, w_hbm, out_ref, q_ref, k_ref, v_ref, g_ref, w_ref, sems):
    copies = [
        pltpu.make_async_copy(source, target, sems.at[i])
        for i, (source, target) in enumerate(
            [(q_hbm, q_ref), (k_hbm, k_ref), (v_hbm, v_ref), (g_hbm, g_ref), (w_hbm, w_ref)]
        )
    ]
    for copy in copies:
        copy.start()
    parts = []
    for i, ref in enumerate((q_ref, k_ref, v_ref)):
        copies[i].wait()
        parts.append(ref[...].astype(F32).T)
    copies[3].wait()
    copies[4].wait()
    parts.append(dot(w_ref[...], g_ref[...], NT).astype(BF16).astype(F32))
    for h in range(HEADS):
        rows = slice(h * HEAD, (h + 1) * HEAD)
        out_ref[h] = jnp.concatenate([part[rows] for part in parts], axis=0).astype(BF16)


def pack(queries, keys, values, out_grad, out_weight):
    width = HEADS * HEAD
    return pl.pallas_call(
        pack_body,
        out_shape=jax.ShapeDtypeStruct((HEADS, 4 * HEAD, ROWS), BF16),
        in_specs=[pl.BlockSpec(memory_space=pltpu.HBM)] * 5,
        out_specs=pl.BlockSpec(memory_space=pltpu.VMEM),
        scratch_shapes=[pltpu.VMEM((ROWS, width), BF16)] * 4
        + [pltpu.VMEM((width, width), BF16), pltpu.SemaphoreType.DMA((5,))],
        compiler_params=pltpu.CompilerParams(vmem_limit_bytes=VMEM_MOST),
        cost_estimate=pl.CostEstimate(flops=10**10, bytes_accessed=0, transcendentals=0),
        name="pack",
    )(queries, keys, values, out_grad, out_weight)


def kept(total, later):
    return jnp.where(later > 0, total, 0.0)


def attend_body(
    me_ref, ext_ref, r_ref, g_ref, att_ref, q_s, b_s, k_s, v_s, kn_s, vn_s, e_s, acc_s, dq_s, dk_s, dv_s,
    top_s, pair_top_s, delta_s, inverse_s, qb_s, kb_s, later_q_s, later_k_s
):
    ends = []
    total = jnp.int32(0)
    for i in range(IMAGES):
        total = total + ext_ref[0, i] * UNIT
        ends.append(total)

    lane = lax.broadcasted_iota(jnp.int32, (IMAGES, ROWS), 1)
    row = lax.broadcasted_iota(jnp.int32, (IMAGES, ROWS), 0)
    nothing = jnp.zeros((128 - PAD, ROWS), F32)
    ones_row = jnp.where(row == 0, 1.0, 0.0)
    zeros_rows = jnp.zeros((IMAGES, ROWS), F32)
    for s in range(HEADS):
        b, half = s // 2, s % 2
        lanes = slice(half * ROWS, (half + 1) * ROWS)
        x = r_ref[s].astype(F32)
        q, k, v, back = (x[j * HEAD : (j + 1) * HEAD] for j in range(4))
        segment = jnp.zeros((IMAGES, ROWS), jnp.int32)
        for end in ends:
            segment = segment + (lane + s * ROWS >= end).astype(jnp.int32)
        here = (segment == row).astype(F32)
        q_s[b, :, lanes] = jnp.concatenate([q, here * -FAR, nothing], axis=0).astype(BF16)
        b_s[b, :, lanes] = jnp.concatenate([back, zeros_rows], axis=0).astype(BF16)
        k_aug = jnp.concatenate([k, 1.0 - here, nothing], axis=0)
        v_aug = jnp.concatenate([v, zeros_rows, nothing], axis=0)
        k_s[b, :, lanes] = k_aug[:PAD].astype(BF16)
        v_s[b, :, lanes] = jnp.concatenate([v, ones_row], axis=0).astype(BF16)
        kn_s[b, lanes, :] = k_aug.T.astype(BF16)
        vn_s[b, lanes, :] = v_aug.T.astype(BF16)

    top_s[...] = jnp.full(top_s.shape, -3e38, F32)

    count = jnp.int32(0)
    reached = jnp.int32(0)
    for qb in range(BLOCKS):
        first, last = qb * BLOCK, qb * BLOCK + BLOCK - 1
        start, stop = jnp.int32(0), jnp.int32(BLOCKS * BLOCK)
        for end in ends:
            start = jnp.maximum(start, jnp.where(end <= first, end, 0))
            stop = jnp.minimum(stop, jnp.where(end > last, end, BLOCKS * BLOCK))
        lo = start // BLOCK
        size = (stop + BLOCK - 1) // BLOCK - lo

        def add_pair(i, carry, qb=qb, lo=lo, base=count, reached=reached):
            qb_s[base + i] = qb
            kb_s[base + i] = lo + i
            later_q_s[base + i] = i
            later_k_s[base + i] = (lo + i < reached).astype(jnp.int32)
            return carry

        lax.fori_loop(0, size, add_pair, 0)
        count = count + size
        reached = lo + size
    for u in range(8):
        qb_s[count + u] = BLOCKS
        kb_s[count + u] = BLOCKS
        later_q_s[count + u] = 0
        later_k_s[count + u] = 0

    def forward(i, carry):
        ats = [8 * i + u for u in range(8)]
        qbs = [qb_s[at] for at in ats]
        kbs = [kb_s[at] for at in ats]
        tops = []
        for at, qb, kb in zip(ats, qbs, kbs):
            scores = dot(kn_s[kb], q_s[qb], NN)
            e_s[at] = scores
            top = jnp.max(scores.reshape(BLOCK // 8, 8, BLOCK), axis=0)
            tops.append(jnp.max(top, axis=0, keepdims=True))
        terms = []
        for at, kb, top in zip(ats, kbs, tops):
            e = jnp.exp2((e_s[at] - top) * (SCALE * LOG2E))
            e_s[at] = e
            pair_top_s[at] = top
            terms.append(dot(v_s[kb], e.astype(BF16), NN))
        for at, qb, top, term in zip(ats, qbs, tops, terms):
            before = top_s[qb]
            after = jnp.maximum(before, top)
            top_s[qb] = after
            acc_s[qb] = kept(acc_s[qb], later_q_s[at]) * jnp.exp2((before - after) * (SCALE * LOG2E)) + term * jnp.exp2(
                (top - after) * (SCALE * LOG2E)
            )
        return carry

    lax.fori_loop(0, (count + 8 - 1) // 8 if True else 0, forward, 0)

    for qb in range(BLOCKS):
        acc = acc_s[qb]
        inverse = 1.0 / acc[HEAD : HEAD + 1]
        attended = (acc[:HEAD] * inverse).astype(BF16)
        for half in range(2):
            apart = (2 * qb + half) ^ me_ref[0]
            place = (apart & 3) + ((apart >> 3) << 2) + ((apart & 4) << 1)
            att_ref[place] = attended[:, half * ROWS : (half + 1) * ROWS]
        back = b_s[qb].astype(F32)
        delta_s[qb] = jnp.sum(back[:HEAD] * attended.astype(F32), axis=0, keepdims=True)
        inverse_s[qb] = inverse

    def backward(i, carry):
        ats = [8 * i + u for u in range(8)]
        qbs = [qb_s[at] for at in ats]
        kbs = [kb_s[at] for at in ats]
        backs, dss = [], []
        for at, qb, kb in zip(ats, qbs, kbs):
            factor = jnp.exp2((pair_top_s[at] - top_s[qb]) * (SCALE * LOG2E)) * inverse_s[qb]
            back = (b_s[qb].astype(F32) * factor).astype(BF16)
            back_wide = jnp.concatenate([back, jnp.zeros((128 - PAD, BLOCK), BF16)], axis=0)
            backs.append(back)
            dss.append((e_s[at] * (dot(vn_s[kb], back_wide, NN) - delta_s[qb] * factor)).astype(BF16))
        dvs, dks, dqs = [], [], []
        for at, qb, kb, back, ds in zip(ats, qbs, kbs, backs, dss):
            dvs.append(dot(back, e_s[at].astype(BF16), NT))
            dks.append(dot(q_s[qb][:PAD], ds, NT))
            dqs.append(dot(k_s[kb], ds, NN))
        for at, qb, kb, dv, dk, dq in zip(ats, qbs, kbs, dvs, dks, dqs):
            dv_s[kb] = kept(dv_s[kb], later_k_s[at]) + dv
            dk_s[kb] = kept(dk_s[kb], later_k_s[at]) + dk
            dq_s[qb] = kept(dq_s[qb], later_q_s[at]) + dq
        return carry

    lax.fori_loop(0, (count + 8 - 1) // 8 if True else 0, backward, 0)

    for s in range(HEADS):
        b, half = s // 2, s % 2
        lanes = slice(half * ROWS, (half + 1) * ROWS)
        g_ref[s] = jnp.concatenate(
            [
                dq_s[b, :HEAD, lanes] * SCALE,
                dk_s[b, :HEAD, lanes] * SCALE,
                dv_s[b, :HEAD, lanes],
            ],
            axis=0,
        ).astype(BF16)


def attend(me, extents, received):
    return pl.pallas_call(
        attend_body,
        out_shape=(
            jax.ShapeDtypeStruct((HEADS, 3 * HEAD, ROWS), BF16),
            jax.ShapeDtypeStruct((HEADS, HEAD, ROWS), BF16),
        ),
        in_specs=[
            pl.BlockSpec(memory_space=pltpu.SMEM),
            pl.BlockSpec(memory_space=pltpu.SMEM),
            pl.BlockSpec(memory_space=pltpu.VMEM),
        ],
        scratch_shapes=[
            pltpu.VMEM((BLOCKS + 1, 128, BLOCK), BF16),
            pltpu.VMEM((BLOCKS + 1, PAD, BLOCK), BF16),
            pltpu.VMEM((BLOCKS + 1, PAD, BLOCK), BF16),
            pltpu.VMEM((BLOCKS + 1, PAD, BLOCK), BF16),
            pltpu.VMEM((BLOCKS + 1, BLOCK, 128), BF16),
            pltpu.VMEM((BLOCKS + 1, BLOCK, 128), BF16),
            pltpu.VMEM((PAIRS, BLOCK, BLOCK), F32),
            pltpu.VMEM((BLOCKS + 1, PAD, BLOCK), F32),
            pltpu.VMEM((BLOCKS + 1, PAD, BLOCK), F32),
            pltpu.VMEM((BLOCKS + 1, PAD, BLOCK), F32),
            pltpu.VMEM((BLOCKS + 1, PAD, BLOCK), F32),
            pltpu.VMEM((BLOCKS + 1, 1, BLOCK), F32),
            pltpu.VMEM((PAIRS, 1, BLOCK), F32),
            pltpu.VMEM((BLOCKS + 1, 1, BLOCK), F32),
            pltpu.VMEM((BLOCKS + 1, 1, BLOCK), F32),
            pltpu.SMEM((PAIRS,), jnp.int32),
            pltpu.SMEM((PAIRS,), jnp.int32),
            pltpu.SMEM((PAIRS,), jnp.int32),
            pltpu.SMEM((PAIRS,), jnp.int32),
        ],
        compiler_params=pltpu.CompilerParams(vmem_limit_bytes=VMEM_LIMIT),
        cost_estimate=pl.CostEstimate(flops=10**10, bytes_accessed=0, transcendentals=0),
        name="attend",
    )(me, extents, received)


def unpack_body(y_ref, dq_ref, dk_ref, dv_ref):
    for j, ref in enumerate((dq_ref, dk_ref, dv_ref)):
        rows = [y_ref[h].astype(F32)[j * HEAD : (j + 1) * HEAD] for h in range(HEADS)]
        ref[...] = jnp.concatenate(rows, axis=0).T.astype(BF16)


def unpack(returned):
    shape = jax.ShapeDtypeStruct((ROWS, HEADS * HEAD), BF16)
    return pl.pallas_call(
        unpack_body,
        out_shape=(shape, shape, shape),
        compiler_params=pltpu.CompilerParams(vmem_limit_bytes=VMEM_LIMIT),
        cost_estimate=pl.CostEstimate(flops=10**11, bytes_accessed=0, transcendentals=0),
        name="unpack",
    )(returned)


def weight_body(tile_ref, mine_ref, got_ref, *refs):
    sources, out_ref, grads, sems = refs[:8], refs[8], refs[9], refs[10]
    copies = [
        pltpu.make_async_copy(source, grads.at[pl.ds(i * ROWS, ROWS)], sems.at[i])
        for i, source in enumerate(sources)
    ]
    for copy in copies:
        copy.start()
    total = jnp.zeros((2 * HEAD, HEADS * HEAD), F32)
    for i in range(0, 8, 2):
        left = jnp.concatenate(
            [
                jnp.concatenate([mine_ref[j], got_ref[j]], axis=0) for j in (i, i + 1)
            ],
            axis=1,
        )
        copies[i].wait()
        copies[i + 1].wait()
        total = total + dot(left, grads[i * ROWS : (i + 2) * ROWS], NN)
    for tile in range(8):
        out_ref[tile_ref[tile]] = total[:, tile * 144 : (tile + 1) * 144].astype(BF16)


def weight_terms(places, mine, got, grads):
    return pl.pallas_call(
        weight_body,
        out_shape=jax.ShapeDtypeStruct((8, 2 * HEAD, 144), BF16),
        in_specs=[pl.BlockSpec(memory_space=pltpu.SMEM)]
        + [pl.BlockSpec(memory_space=pltpu.VMEM)] * 2
        + [pl.BlockSpec(memory_space=pl.ANY)] * 8,
        out_specs=pl.BlockSpec(memory_space=pltpu.VMEM),
        scratch_shapes=[
            pltpu.VMEM((8 * ROWS, HEADS * HEAD), BF16),
            pltpu.SemaphoreType.DMA((8,)),
        ],
        compiler_params=pltpu.CompilerParams(vmem_limit_bytes=VMEM_LIMIT),
        cost_estimate=pl.CostEstimate(flops=10**9, bytes_accessed=0, transcendentals=0),
        name="weight_terms",
    )(places, mine, got, *grads)


def swap(x, axis, size, apart):
    return lax.ppermute(x, axis, [(i, i ^ apart) for i in range(size)])


def local(queries, keys, values, out_grad, out_weight, extents):
    me = lax.axis_index("seq")
    part = lax.axis_index("dp")

    sent = pack(queries, keys, values, out_grad, out_weight)
    received = lax.all_to_all(sent, "seq", 0, 0, tiled=True)
    late, received = lax.optimization_barrier((out_grad, received))
    far = [out_grad] + [swap(late, "seq", HEADS, apart) for apart in (2, 8, 10)]
    near = [swap(x, "seq", HEADS, 1) for x in far]
    out_grads = [x for pair in zip(far, near) for x in pair]

    grads, attended = attend(me[None].astype(jnp.int32), extents, received)
    got = swap(attended[8:], "seq", HEADS, 4)
    returned = lax.all_to_all(grads, "seq", 0, 0, tiled=True)

    x_lo, y = part // 4, part % 4
    tile = jnp.arange(8, dtype=jnp.int32)
    places = ((tile // 4) ^ x_lo) + 2 * ((tile % 4) ^ y)
    terms = weight_terms(places.astype(jnp.int32), attended[:8], got, out_grads)
    total = terms[:2].astype(F32)
    for apart in (1, 2, 3):
        total = total + swap(terms[2 * apart : 2 * apart + 2], "dp", 8, apart).astype(F32)
    weight_grad = total[0, :HEAD]
    for x_apart, z_apart in ((1, 0), (0, 1), (1, 1)):
        give = total[x_apart, z_apart * HEAD : (z_apart + 1) * HEAD].astype(BF16)
        pairs = [(i, i ^ (64 * x_apart + 4 * z_apart)) for i in range(128)]
        weight_grad = weight_grad + lax.ppermute(give, ("dp", "seq"), pairs).astype(F32)

    query_grad, key_grad, value_grad = unpack(returned)
    return query_grad, key_grad, value_grad, weight_grad


def solution(mesh):
    tokens = P(("dp", "seq"), None)
    return jax.shard_map(
        local,
        mesh=mesh,
        in_specs=(tokens, tokens, tokens, tokens, P(), P("dp", None)),
        out_specs=(tokens, tokens, tokens, P("seq", "dp")),
        check_vma=False,
    )
```

```python
import functools

import jax
import jax.numpy as jnp
from jax import lax
from jax.experimental import pallas as pl
from jax.experimental.pallas import tpu as pltpu
from jax.sharding import PartitionSpec as P

HEADS = 16
HEAD = 72
IMAGES = 8
UNIT = 64
ROWS = 128
BLOCK = 256
BLOCKS = 8
GROUP = 4
PAIRS = BLOCKS * BLOCKS + 3 * GROUP
TILE = 144
REST = TILE - ROWS
STRIP = 24
PARTS = 4
PAD = 80
SCALE = HEAD**-0.5
LOG2E = 1.4426950408889634
FAR = 16384.0
F32 = jnp.float32
BF16 = jnp.bfloat16
VMEM_SOME = 12 << 20
VMEM_MORE = 36 << 20
VMEM_MOST = (64 << 20) - (128 << 10)

NN = (((1,), (0,)), ((), ()))
NT = (((1,), (1,)), ((), ()))


def dot(a, b, dims):
    return lax.dot_general(a, b, dims, preferred_element_type=F32)


def pack_body(
    q_hbm, k_hbm, v_hbm, g_hbm, w_hbm, out_hbm, q_ref, k_ref, v_ref, g_ref, w_ref, out_ref, sems, out_sems
):
    width = HEADS * HEAD // PARTS
    heads = HEADS // PARTS
    ins = [
        pltpu.make_async_copy(source, target, sems.at[i])
        for i, (source, target) in enumerate(
            [(q_hbm, q_ref), (k_hbm, k_ref), (v_hbm, v_ref), (g_hbm, g_ref)]
            + [(w_hbm.at[pl.ds(p * width, width)], w_ref.at[p]) for p in range(PARTS)]
        )
    ]
    for copy in ins:
        copy.start()
    turned = []
    for i, ref in enumerate((q_ref, k_ref, v_ref)):
        ins[i].wait()
        turned.append(ref[...].astype(F32).T)
    ins[3].wait()
    outs = []
    for p in range(PARTS):
        ins[4 + p].wait()
        back = dot(w_ref[p], g_ref[...], NT).astype(BF16).astype(F32)
        for i in range(heads):
            h = p * heads + i
            rows = [x[h * HEAD : (h + 1) * HEAD] for x in turned]
            rows.append(back[i * HEAD : (i + 1) * HEAD])
            out_ref[h] = jnp.concatenate(rows, axis=0).astype(BF16)
        part = pl.ds(p * heads, heads)
        outs.append(pltpu.make_async_copy(out_ref.at[part], out_hbm.at[part], out_sems.at[p]))
        outs[p].start()
    for copy in outs:
        copy.wait()


def pack(queries, keys, values, out_grad, out_weight):
    width = HEADS * HEAD
    shape = (HEADS, 4 * HEAD, ROWS)
    return pl.pallas_call(
        pack_body,
        out_shape=jax.ShapeDtypeStruct(shape, BF16),
        in_specs=[pl.BlockSpec(memory_space=pltpu.HBM)] * 5,
        out_specs=pl.BlockSpec(memory_space=pl.ANY),
        scratch_shapes=[pltpu.VMEM((ROWS, width), BF16)] * 4
        + [
            pltpu.VMEM((PARTS, width // PARTS, width), BF16),
            pltpu.VMEM(shape, BF16),
            pltpu.SemaphoreType.DMA((4 + PARTS,)),
            pltpu.SemaphoreType.DMA((PARTS,)),
        ],
        compiler_params=pltpu.CompilerParams(vmem_limit_bytes=VMEM_MOST),
        cost_estimate=pl.CostEstimate(flops=10**10, bytes_accessed=0, transcendentals=0),
        name="pack",
    )(queries, keys, values, out_grad, out_weight)


def kept(total, later):
    return jnp.where(later > 0, total, 0.0)


def attend_body(
    me_ref, ext_ref, r_ref, g_ref, mine_ref, give_ref, q_s, b_s, k_s, v_s, kn_s, vn_s, e_s, acc_s, dq_s, dk_s, dv_s,
    top_s, pair_top_s, delta_s, inverse_s, qb_s, kb_s, later_q_s, later_k_s,
    even_s, odd_s, ds_even_s, ds_odd_s, back_even_s, back_odd_s
):
    ends = []
    total = jnp.int32(0)
    for i in range(IMAGES):
        total = total + ext_ref[0, i] * UNIT
        ends.append(total)

    lane = lax.broadcasted_iota(jnp.int32, (IMAGES, ROWS), 1)
    row = lax.broadcasted_iota(jnp.int32, (IMAGES, ROWS), 0)
    nothing = jnp.zeros((128 - PAD, ROWS), F32)
    ones_row = jnp.where(row == 0, 1.0, 0.0)
    zeros_rows = jnp.zeros((IMAGES, ROWS), F32)
    for s in range(HEADS):
        b, half = s // 2, s % 2
        lanes = slice(half * ROWS, (half + 1) * ROWS)
        x = r_ref[s].astype(F32)
        q, k, v, back = (x[j * HEAD : (j + 1) * HEAD] for j in range(4))
        segment = jnp.zeros((IMAGES, ROWS), jnp.int32)
        for end in ends:
            segment = segment + (lane + s * ROWS >= end).astype(jnp.int32)
        here = (segment == row).astype(F32)
        q_s[b, :, lanes] = jnp.concatenate([q, here * -FAR, nothing], axis=0).astype(BF16)
        b_s[b, :, lanes] = jnp.concatenate([back, zeros_rows], axis=0).astype(BF16)
        k_aug = jnp.concatenate([k, 1.0 - here, nothing], axis=0)
        v_aug = jnp.concatenate([v, zeros_rows, nothing], axis=0)
        k_s[b, :, lanes] = k_aug[:PAD].astype(BF16)
        v_s[b, :, lanes] = jnp.concatenate([v, ones_row], axis=0).astype(BF16)
        kn_s[b, lanes, :] = k_aug.T.astype(BF16)
        vn_s[b, lanes, :] = v_aug.T.astype(BF16)

    top_s[...] = jnp.full(top_s.shape, -3e38, F32)

    count = jnp.int32(0)
    reached = jnp.int32(0)
    for qb in range(BLOCKS):
        first, last = qb * BLOCK, qb * BLOCK + BLOCK - 1
        start, stop = jnp.int32(0), jnp.int32(BLOCKS * BLOCK)
        for end in ends:
            start = jnp.maximum(start, jnp.where(end <= first, end, 0))
            stop = jnp.minimum(stop, jnp.where(end > last, end, BLOCKS * BLOCK))
        lo = start // BLOCK
        size = (stop + BLOCK - 1) // BLOCK - lo

        def add_pair(i, carry, qb=qb, lo=lo, base=count, reached=reached):
            qb_s[base + i] = qb
            kb_s[base + i] = lo + i
            later_q_s[base + i] = i
            later_k_s[base + i] = (lo + i < reached).astype(jnp.int32)
            return carry

        lax.fori_loop(0, size, add_pair, 0)
        count = count + size
        reached = lo + size
    for u in range(3 * GROUP):
        qb_s[count + u] = BLOCKS
        kb_s[count + u] = BLOCKS
        later_q_s[count + u] = 0
        later_k_s[count + u] = 0

    def score(at, ref, u):
        scores = dot(kn_s[kb_s[at]][:, :PAD], q_s[qb_s[at]][:PAD], NN)
        ref[u] = scores
        top = jnp.max(scores.reshape(BLOCK // 8, 8, BLOCK), axis=0)
        pair_top_s[at] = jnp.max(top, axis=0, keepdims=True)

    def soften(at, ref, u):
        e = jnp.exp2((ref[u] - pair_top_s[at]) * (SCALE * LOG2E))
        e_s[at] = e
        return dot(v_s[kb_s[at]], e.astype(BF16), NN)

    def gather(at, term):
        qb, top = qb_s[at], pair_top_s[at]
        before = top_s[qb]
        after = jnp.maximum(before, top)
        top_s[qb] = after
        acc_s[qb] = kept(acc_s[qb], later_q_s[at]) * jnp.exp2(
            (before - after) * (SCALE * LOG2E)
        ) + term * jnp.exp2((top - after) * (SCALE * LOG2E))

    def forward(i, carry):
        for first, now, ahead in ((2 * i, even_s, odd_s), (2 * i + 1, odd_s, even_s)):
            terms = []
            for u in range(GROUP):
                score((first + 1) * GROUP + u, ahead, u)
                terms.append(soften(first * GROUP + u, now, u))
            for u in range(GROUP):
                gather(first * GROUP + u, terms[u])
        return carry

    rounds = (count + 2 * GROUP - 1) // (2 * GROUP)
    for u in range(GROUP):
        score(u, even_s, u)
    lax.fori_loop(0, rounds, forward, 0)

    for qb in range(BLOCKS):
        acc = acc_s[qb]
        inverse = 1.0 / acc[HEAD : HEAD + 1]
        attended = (acc[:HEAD] * inverse).astype(BF16)
        for half in range(2):
            apart = (2 * qb + half) ^ me_ref[0]
            place = (apart & 3) + ((apart >> 3) << 2)
            rows = attended[:, half * ROWS : (half + 1) * ROWS]

            @pl.when(apart & 4 == 0)
            def _(place=place, rows=rows):
                mine_ref[place] = rows

            @pl.when(apart & 4 != 0)
            def _(place=place, rows=rows):
                give_ref[place] = rows

        back = b_s[qb].astype(F32)
        delta_s[qb] = jnp.sum(back[:HEAD] * attended.astype(F32), axis=0, keepdims=True)
        inverse_s[qb] = inverse

    def differ(at, ds_ref, back_ref, u):
        qb = qb_s[at]
        factor = jnp.exp2((pair_top_s[at] - top_s[qb]) * (SCALE * LOG2E)) * inverse_s[qb]
        back = (b_s[qb].astype(F32) * factor).astype(BF16)
        back_ref[u] = back
        dprobs = dot(vn_s[kb_s[at]][:, :PAD], back, NN)
        ds_ref[u] = (e_s[at] * (dprobs - delta_s[qb] * factor)).astype(BF16)

    def products(at, ds_ref, back_ref, u):
        dv = dot(back_ref[u], e_s[at].astype(BF16), NT)
        dk = dot(q_s[qb_s[at]][:PAD], ds_ref[u], NT)
        dq = dot(k_s[kb_s[at]], ds_ref[u], NN)
        return dv, dk, dq

    def collect(at, dv, dk, dq):
        qb, kb = qb_s[at], kb_s[at]
        dv_s[kb] = kept(dv_s[kb], later_k_s[at]) + dv
        dk_s[kb] = kept(dk_s[kb], later_k_s[at]) + dk
        dq_s[qb] = kept(dq_s[qb], later_q_s[at]) + dq

    def backward(i, carry):
        for first, now, ahead in ((2 * i, even, odd), (2 * i + 1, odd, even)):
            terms = []
            for u in range(GROUP):
                differ((first + 1) * GROUP + u, *ahead, u)
                terms.append(products(first * GROUP + u, *now, u))
            for u in range(GROUP):
                collect(first * GROUP + u, *terms[u])
        return carry

    even, odd = (ds_even_s, back_even_s), (ds_odd_s, back_odd_s)
    for u in range(GROUP):
        differ(u, *even, u)
    lax.fori_loop(0, rounds, backward, 0)

    for s in range(HEADS):
        b, half = s // 2, s % 2
        lanes = slice(half * ROWS, (half + 1) * ROWS)
        g_ref[s] = jnp.concatenate(
            [
                dq_s[b, :HEAD, lanes] * SCALE,
                dk_s[b, :HEAD, lanes] * SCALE,
                dv_s[b, :HEAD, lanes],
            ],
            axis=0,
        ).astype(BF16)


def attend(me, extents, received):
    return pl.pallas_call(
        attend_body,
        out_shape=(
            jax.ShapeDtypeStruct((HEADS, 3 * HEAD, ROWS), BF16),
            jax.ShapeDtypeStruct((HEADS // 2, HEAD, ROWS), BF16),
            jax.ShapeDtypeStruct((HEADS // 2, HEAD, ROWS), BF16),
        ),
        in_specs=[
            pl.BlockSpec(memory_space=pltpu.SMEM),
            pl.BlockSpec(memory_space=pltpu.SMEM),
            pl.BlockSpec(memory_space=pltpu.VMEM),
        ],
        scratch_shapes=[
            pltpu.VMEM((BLOCKS + 1, 128, BLOCK), BF16),
            pltpu.VMEM((BLOCKS + 1, PAD, BLOCK), BF16),
            pltpu.VMEM((BLOCKS + 1, PAD, BLOCK), BF16),
            pltpu.VMEM((BLOCKS + 1, PAD, BLOCK), BF16),
            pltpu.VMEM((BLOCKS + 1, BLOCK, 128), BF16),
            pltpu.VMEM((BLOCKS + 1, BLOCK, 128), BF16),
            pltpu.VMEM((PAIRS, BLOCK, BLOCK), F32),
            pltpu.VMEM((BLOCKS + 1, PAD, BLOCK), F32),
            pltpu.VMEM((BLOCKS + 1, PAD, BLOCK), F32),
            pltpu.VMEM((BLOCKS + 1, PAD, BLOCK), F32),
            pltpu.VMEM((BLOCKS + 1, PAD, BLOCK), F32),
            pltpu.VMEM((BLOCKS + 1, 1, BLOCK), F32),
            pltpu.VMEM((PAIRS, 1, BLOCK), F32),
            pltpu.VMEM((BLOCKS + 1, 1, BLOCK), F32),
            pltpu.VMEM((BLOCKS + 1, 1, BLOCK), F32),
            pltpu.SMEM((PAIRS,), jnp.int32),
            pltpu.SMEM((PAIRS,), jnp.int32),
            pltpu.SMEM((PAIRS,), jnp.int32),
            pltpu.SMEM((PAIRS,), jnp.int32),
            pltpu.VMEM((GROUP, BLOCK, BLOCK), F32),
            pltpu.VMEM((GROUP, BLOCK, BLOCK), F32),
            pltpu.VMEM((GROUP, BLOCK, BLOCK), BF16),
            pltpu.VMEM((GROUP, BLOCK, BLOCK), BF16),
            pltpu.VMEM((GROUP, PAD, BLOCK), BF16),
            pltpu.VMEM((GROUP, PAD, BLOCK), BF16),
        ],
        compiler_params=pltpu.CompilerParams(vmem_limit_bytes=VMEM_MORE),
        cost_estimate=pl.CostEstimate(flops=10**10, bytes_accessed=0, transcendentals=0),
        name="attend",
    )(me, extents, received)


def unpack_body(y_ref, dq_ref, dk_ref, dv_ref):
    for j, ref in enumerate((dq_ref, dk_ref, dv_ref)):
        rows = [y_ref[h].astype(F32)[j * HEAD : (j + 1) * HEAD] for h in range(HEADS)]
        ref[...] = jnp.concatenate(rows, axis=0).T.astype(BF16)


def unpack(returned):
    shape = jax.ShapeDtypeStruct((ROWS, HEADS * HEAD), BF16)
    return pl.pallas_call(
        unpack_body,
        out_shape=(shape, shape, shape),
        compiler_params=pltpu.CompilerParams(vmem_limit_bytes=VMEM_SOME),
        cost_estimate=pl.CostEstimate(flops=10**11, bytes_accessed=0, transcendentals=0),
        name="unpack",
    )(returned)


def weight_body(tile_ref, mine_ref, got_ref, *refs):
    sources, out_ref, grads, sems = refs[:8], refs[8], refs[9], refs[10]
    copies = [
        pltpu.make_async_copy(source, grads.at[pl.ds(i * ROWS, ROWS)], sems.at[i])
        for i, source in enumerate(sources)
    ]
    for copy in copies:
        copy.start()
    total = jnp.zeros((2 * HEAD, HEADS * HEAD), F32)
    for i in range(0, 8, 2):
        left = jnp.concatenate(
            [
                jnp.concatenate([mine_ref[j], got_ref[j]], axis=0) for j in (i, i + 1)
            ],
            axis=1,
        )
        copies[i].wait()
        copies[i + 1].wait()
        total = total + dot(left, grads[i * ROWS : (i + 2) * ROWS], NN)
    empty = jnp.zeros((STRIP, ROWS - 3 * REST), F32)
    for tile in range(8):
        for head in range(2):
            part = total[head * HEAD : (head + 1) * HEAD, tile * TILE : (tile + 1) * TILE]
            rest = [part[i * STRIP : (i + 1) * STRIP, ROWS:] for i in range(3)]
            rest = jnp.concatenate(rest + [empty], axis=1)
            out_ref[tile_ref[tile], head] = jnp.concatenate([part[:, :ROWS], rest], axis=0).astype(BF16)


def weight_terms(places, mine, got, grads):
    return pl.pallas_call(
        weight_body,
        out_shape=jax.ShapeDtypeStruct((8, 2, HEAD + STRIP, ROWS), BF16),
        in_specs=[pl.BlockSpec(memory_space=pltpu.SMEM)]
        + [pl.BlockSpec(memory_space=pltpu.VMEM)] * 2
        + [pl.BlockSpec(memory_space=pl.ANY)] * 8,
        out_specs=pl.BlockSpec(memory_space=pltpu.VMEM),
        scratch_shapes=[
            pltpu.VMEM((8 * ROWS, HEADS * HEAD), BF16),
            pltpu.SemaphoreType.DMA((8,)),
        ],
        compiler_params=pltpu.CompilerParams(vmem_limit_bytes=VMEM_SOME),
        cost_estimate=pl.CostEstimate(flops=10**9, bytes_accessed=0, transcendentals=0),
        name="weight_terms",
    )(places, mine, got, *grads)


def finish_body(own_ref, *refs):
    total = own_ref[...]
    for ref in refs[:-1]:
        total = total + ref[...].astype(F32)
    rest = [total[HEAD:, i * REST : (i + 1) * REST] for i in range(3)]
    refs[-1][...] = jnp.concatenate([total[:HEAD], jnp.concatenate(rest, axis=0)], axis=1)


def finish(own, others):
    return pl.pallas_call(
        finish_body,
        out_shape=jax.ShapeDtypeStruct((HEAD, TILE), F32),
        compiler_params=pltpu.CompilerParams(vmem_limit_bytes=VMEM_SOME),
        name="finish",
    )(own, *others)


def swap(x, axis, size, apart):
    return lax.ppermute(x, axis, [(i, i ^ apart) for i in range(size)])


def local(queries, keys, values, out_grad, out_weight, extents):
    me = lax.axis_index("seq")
    part = lax.axis_index("dp")

    sent = pack(queries, keys, values, out_grad, out_weight)
    received = lax.all_to_all(sent, "seq", 0, 0, tiled=True)
    late, received = lax.optimization_barrier((out_grad, received))
    far = [out_grad] + [swap(late, "seq", HEADS, apart) for apart in (2, 8, 10)]
    grads, mine, give = attend(me[None].astype(jnp.int32), extents, received)
    got = swap(give, "seq", HEADS, 4)
    _, *far = lax.optimization_barrier((give, *far))
    near = [swap(x, "seq", HEADS, 1) for x in far]
    out_grads = [x for pair in zip(far, near) for x in pair]
    returned = lax.all_to_all(grads, "seq", 0, 0, tiled=True)

    x_lo, y = part // 4, part % 4
    tile = jnp.arange(8, dtype=jnp.int32)
    places = ((tile // 4) ^ x_lo) + 2 * ((tile % 4) ^ y)
    terms = weight_terms(places.astype(jnp.int32), mine, got, out_grads)
    total = terms[:2].astype(F32)
    for apart in (1, 2, 3):
        total = total + swap(terms[2 * apart : 2 * apart + 2], "dp", 8, apart).astype(F32)
    last = []
    for x_apart, z_apart in ((1, 0), (0, 1), (1, 1)):
        pairs = [(i, i ^ (64 * x_apart + 4 * z_apart)) for i in range(128)]
        last.append(lax.ppermute(total[x_apart, z_apart].astype(BF16), ("dp", "seq"), pairs))
    query_grad, key_grad, value_grad = unpack(returned)
    value_grad, *last = lax.optimization_barrier((value_grad, *last))
    weight_grad = finish(total[0, 0], last)
    return query_grad, key_grad, value_grad, weight_grad


def solution(mesh):
    tokens = P(("dp", "seq"), None)
    return jax.shard_map(
        local,
        mesh=mesh,
        in_specs=(tokens, tokens, tokens, tokens, P(), P("dp", None)),
        out_specs=(tokens, tokens, tokens, P("seq", "dp")),
        check_vma=False,
    )
```

```python
import functools

import jax
import jax.numpy as jnp
from jax import lax
from jax.experimental import pallas as pl
from jax.experimental.pallas import tpu as pltpu
from jax.sharding import PartitionSpec as P

HEADS = 16
HEAD = 72
IMAGES = 8
UNIT = 64
ROWS = 128
BLOCK = 256
BLOCKS = 8
GROUP = 4
PAIRS = BLOCKS * BLOCKS + 3 * GROUP
TILE = 144
REST = TILE - ROWS
STRIP = 24
PARTS = 4
PAD = 80
SCALE = HEAD**-0.5
LOG2E = 1.4426950408889634
FAR = 16384.0
F32 = jnp.float32
BF16 = jnp.bfloat16
VMEM_SOME = 12 << 20
VMEM_MORE = 36 << 20
VMEM_MOST = (64 << 20) - (128 << 10)

NN = (((1,), (0,)), ((), ()))
NT = (((1,), (1,)), ((), ()))


def dot(a, b, dims):
    return lax.dot_general(a, b, dims, preferred_element_type=F32)


def pack_body(
    q_hbm, k_hbm, v_hbm, g_hbm, w_hbm, out_hbm, q_ref, k_ref, v_ref, g_ref, w_ref, out_ref, sems, out_sems
):
    width = HEADS * HEAD // PARTS
    heads = HEADS // PARTS
    ins = [
        pltpu.make_async_copy(source, target, sems.at[i])
        for i, (source, target) in enumerate(
            [(q_hbm, q_ref), (k_hbm, k_ref), (v_hbm, v_ref), (g_hbm, g_ref)]
            + [(w_hbm.at[pl.ds(p * width, width)], w_ref.at[p]) for p in range(PARTS)]
        )
    ]
    for copy in ins:
        copy.start()
    turned = []
    for i, ref in enumerate((q_ref, k_ref, v_ref)):
        ins[i].wait()
        turned.append(ref[...].astype(F32).T)
    ins[3].wait()
    outs = []
    for p in range(PARTS):
        ins[4 + p].wait()
        back = dot(w_ref[p], g_ref[...], NT).astype(BF16).astype(F32)
        for i in range(heads):
            h = p * heads + i
            rows = [x[h * HEAD : (h + 1) * HEAD] for x in turned]
            rows.append(back[i * HEAD : (i + 1) * HEAD])
            out_ref[h] = jnp.concatenate(rows, axis=0).astype(BF16)
        part = pl.ds(p * heads, heads)
        outs.append(pltpu.make_async_copy(out_ref.at[part], out_hbm.at[part], out_sems.at[p]))
        outs[p].start()
    for copy in outs:
        copy.wait()


def pack(queries, keys, values, out_grad, out_weight):
    width = HEADS * HEAD
    shape = (HEADS, 4 * HEAD, ROWS)
    return pl.pallas_call(
        pack_body,
        out_shape=jax.ShapeDtypeStruct(shape, BF16),
        in_specs=[pl.BlockSpec(memory_space=pltpu.HBM)] * 5,
        out_specs=pl.BlockSpec(memory_space=pl.ANY),
        scratch_shapes=[pltpu.VMEM((ROWS, width), BF16)] * 4
        + [
            pltpu.VMEM((PARTS, width // PARTS, width), BF16),
            pltpu.VMEM(shape, BF16),
            pltpu.SemaphoreType.DMA((4 + PARTS,)),
            pltpu.SemaphoreType.DMA((PARTS,)),
        ],
        compiler_params=pltpu.CompilerParams(vmem_limit_bytes=VMEM_MOST),
        cost_estimate=pl.CostEstimate(flops=10**10, bytes_accessed=0, transcendentals=0),
        name="pack",
    )(queries, keys, values, out_grad, out_weight)


def kept(total, later):
    return jnp.where(later > 0, total, 0.0)


def attend_body(
    me_ref, ext_ref, r_ref, g_ref, mine_hbm, give_ref, q_s, b_s, k_s, v_s, kn_s, vn_s, e_s, acc_s, dq_s, dk_s, dv_s,
    top_s, pair_top_s, delta_s, inverse_s, qb_s, kb_s, later_q_s, later_k_s,
    even_s, odd_s, ds_even_s, ds_odd_s, back_even_s, back_odd_s, mine_ref, mine_sem
):
    ends = []
    total = jnp.int32(0)
    for i in range(IMAGES):
        total = total + ext_ref[0, i] * UNIT
        ends.append(total)

    lane = lax.broadcasted_iota(jnp.int32, (IMAGES, ROWS), 1)
    row = lax.broadcasted_iota(jnp.int32, (IMAGES, ROWS), 0)
    nothing = jnp.zeros((128 - PAD, ROWS), F32)
    ones_row = jnp.where(row == 0, 1.0, 0.0)
    zeros_rows = jnp.zeros((IMAGES, ROWS), F32)
    for s in range(HEADS):
        b, half = s // 2, s % 2
        lanes = slice(half * ROWS, (half + 1) * ROWS)
        x = r_ref[s].astype(F32)
        q, k, v, back = (x[j * HEAD : (j + 1) * HEAD] for j in range(4))
        segment = jnp.zeros((IMAGES, ROWS), jnp.int32)
        for end in ends:
            segment = segment + (lane + s * ROWS >= end).astype(jnp.int32)
        here = (segment == row).astype(F32)
        q_s[b, :, lanes] = jnp.concatenate([q, here * -FAR, nothing], axis=0).astype(BF16)
        b_s[b, :, lanes] = jnp.concatenate([back, zeros_rows], axis=0).astype(BF16)
        k_aug = jnp.concatenate([k, 1.0 - here, nothing], axis=0)
        v_aug = jnp.concatenate([v, zeros_rows, nothing], axis=0)
        k_s[b, :, lanes] = k_aug[:PAD].astype(BF16)
        v_s[b, :, lanes] = jnp.concatenate([v, ones_row], axis=0).astype(BF16)
        kn_s[b, lanes, :] = k_aug.T.astype(BF16)
        vn_s[b, lanes, :] = v_aug.T.astype(BF16)

    top_s[...] = jnp.full(top_s.shape, -3e38, F32)

    count = jnp.int32(0)
    reached = jnp.int32(0)
    for qb in range(BLOCKS):
        first, last = qb * BLOCK, qb * BLOCK + BLOCK - 1
        start, stop = jnp.int32(0), jnp.int32(BLOCKS * BLOCK)
        for end in ends:
            start = jnp.maximum(start, jnp.where(end <= first, end, 0))
            stop = jnp.minimum(stop, jnp.where(end > last, end, BLOCKS * BLOCK))
        lo = start // BLOCK
        size = (stop + BLOCK - 1) // BLOCK - lo

        def add_pair(i, carry, qb=qb, lo=lo, base=count, reached=reached):
            qb_s[base + i] = qb
            kb_s[base + i] = lo + i
            later_q_s[base + i] = i
            later_k_s[base + i] = (lo + i < reached).astype(jnp.int32)
            return carry

        lax.fori_loop(0, size, add_pair, 0)
        count = count + size
        reached = lo + size
    for u in range(3 * GROUP):
        qb_s[count + u] = BLOCKS
        kb_s[count + u] = BLOCKS
        later_q_s[count + u] = 0
        later_k_s[count + u] = 0

    def score(at, ref, u):
        scores = dot(kn_s[kb_s[at]][:, :PAD], q_s[qb_s[at]][:PAD], NN)
        ref[u] = scores
        top = jnp.max(scores.reshape(BLOCK // 8, 8, BLOCK), axis=0)
        pair_top_s[at] = jnp.max(top, axis=0, keepdims=True)

    def soften(at, ref, u):
        e = jnp.exp2((ref[u] - pair_top_s[at]) * (SCALE * LOG2E))
        e_s[at] = e
        return dot(v_s[kb_s[at]], e.astype(BF16), NN)

    def gather(at, term):
        qb, top = qb_s[at], pair_top_s[at]
        before = top_s[qb]
        after = jnp.maximum(before, top)
        top_s[qb] = after
        acc_s[qb] = kept(acc_s[qb], later_q_s[at]) * jnp.exp2(
            (before - after) * (SCALE * LOG2E)
        ) + term * jnp.exp2((top - after) * (SCALE * LOG2E))

    def forward(i, carry):
        for first, now, ahead in ((2 * i, even_s, odd_s), (2 * i + 1, odd_s, even_s)):
            terms = []
            for u in range(GROUP):
                score((first + 1) * GROUP + u, ahead, u)
                terms.append(soften(first * GROUP + u, now, u))
            for u in range(GROUP):
                gather(first * GROUP + u, terms[u])
        return carry

    rounds = (count + 2 * GROUP - 1) // (2 * GROUP)
    for u in range(GROUP):
        score(u, even_s, u)
    lax.fori_loop(0, rounds, forward, 0)

    for qb in range(BLOCKS):
        acc = acc_s[qb]
        inverse = 1.0 / acc[HEAD : HEAD + 1]
        attended = (acc[:HEAD] * inverse).astype(BF16)
        for half in range(2):
            apart = (2 * qb + half) ^ me_ref[0]
            place = (apart & 3) + ((apart >> 3) << 2)
            rows = attended[:, half * ROWS : (half + 1) * ROWS]

            @pl.when(apart & 4 == 0)
            def _(place=place, rows=rows):
                mine_ref[place] = rows

            @pl.when(apart & 4 != 0)
            def _(place=place, rows=rows):
                give_ref[place] = rows

        back = b_s[qb].astype(F32)
        delta_s[qb] = jnp.sum(back[:HEAD] * attended.astype(F32), axis=0, keepdims=True)
        inverse_s[qb] = inverse

    keep = pltpu.make_async_copy(mine_ref, mine_hbm, mine_sem)
    keep.start()

    def differ(at, ds_ref, back_ref, u):
        qb = qb_s[at]
        factor = jnp.exp2((pair_top_s[at] - top_s[qb]) * (SCALE * LOG2E)) * inverse_s[qb]
        back = (b_s[qb].astype(F32) * factor).astype(BF16)
        back_ref[u] = back
        dprobs = dot(vn_s[kb_s[at]][:, :PAD], back, NN)
        ds_ref[u] = (e_s[at] * (dprobs - delta_s[qb] * factor)).astype(BF16)

    def products(at, ds_ref, back_ref, u):
        dv = dot(back_ref[u], e_s[at].astype(BF16), NT)
        dk = dot(q_s[qb_s[at]][:PAD], ds_ref[u], NT)
        dq = dot(k_s[kb_s[at]], ds_ref[u], NN)
        return dv, dk, dq

    def collect(at, dv, dk, dq):
        qb, kb = qb_s[at], kb_s[at]
        dv_s[kb] = kept(dv_s[kb], later_k_s[at]) + dv
        dk_s[kb] = kept(dk_s[kb], later_k_s[at]) + dk
        dq_s[qb] = kept(dq_s[qb], later_q_s[at]) + dq

    def backward(i, carry):
        for first, now, ahead in ((2 * i, even, odd), (2 * i + 1, odd, even)):
            terms = []
            for u in range(GROUP):
                differ((first + 1) * GROUP + u, *ahead, u)
                terms.append(products(first * GROUP + u, *now, u))
            for u in range(GROUP):
                collect(first * GROUP + u, *terms[u])
        return carry

    even, odd = (ds_even_s, back_even_s), (ds_odd_s, back_odd_s)
    for u in range(GROUP):
        differ(u, *even, u)
    lax.fori_loop(0, rounds, backward, 0)

    for s in range(HEADS):
        b, half = s // 2, s % 2
        lanes = slice(half * ROWS, (half + 1) * ROWS)
        g_ref[s] = jnp.concatenate(
            [
                dq_s[b, :HEAD, lanes] * SCALE,
                dk_s[b, :HEAD, lanes] * SCALE,
                dv_s[b, :HEAD, lanes],
            ],
            axis=0,
        ).astype(BF16)
    keep.wait()


def attend(me, extents, received):
    return pl.pallas_call(
        attend_body,
        out_shape=(
            jax.ShapeDtypeStruct((HEADS, 3 * HEAD, ROWS), BF16),
            jax.ShapeDtypeStruct((HEADS // 2, HEAD, ROWS), BF16),
            jax.ShapeDtypeStruct((HEADS // 2, HEAD, ROWS), BF16),
        ),
        in_specs=[
            pl.BlockSpec(memory_space=pltpu.SMEM),
            pl.BlockSpec(memory_space=pltpu.SMEM),
            pl.BlockSpec(memory_space=pltpu.VMEM),
        ],
        out_specs=(
            pl.BlockSpec(memory_space=pltpu.VMEM),
            pl.BlockSpec(memory_space=pltpu.HBM),
            pl.BlockSpec(memory_space=pltpu.VMEM),
        ),
        scratch_shapes=[
            pltpu.VMEM((BLOCKS + 1, 128, BLOCK), BF16),
            pltpu.VMEM((BLOCKS + 1, PAD, BLOCK), BF16),
            pltpu.VMEM((BLOCKS + 1, PAD, BLOCK), BF16),
            pltpu.VMEM((BLOCKS + 1, PAD, BLOCK), BF16),
            pltpu.VMEM((BLOCKS + 1, BLOCK, 128), BF16),
            pltpu.VMEM((BLOCKS + 1, BLOCK, 128), BF16),
            pltpu.VMEM((PAIRS, BLOCK, BLOCK), F32),
            pltpu.VMEM((BLOCKS + 1, PAD, BLOCK), F32),
            pltpu.VMEM((BLOCKS + 1, PAD, BLOCK), F32),
            pltpu.VMEM((BLOCKS + 1, PAD, BLOCK), F32),
            pltpu.VMEM((BLOCKS + 1, PAD, BLOCK), F32),
            pltpu.VMEM((BLOCKS + 1, 1, BLOCK), F32),
            pltpu.VMEM((PAIRS, 1, BLOCK), F32),
            pltpu.VMEM((BLOCKS + 1, 1, BLOCK), F32),
            pltpu.VMEM((BLOCKS + 1, 1, BLOCK), F32),
            pltpu.SMEM((PAIRS,), jnp.int32),
            pltpu.SMEM((PAIRS,), jnp.int32),
            pltpu.SMEM((PAIRS,), jnp.int32),
            pltpu.SMEM((PAIRS,), jnp.int32),
            pltpu.VMEM((GROUP, BLOCK, BLOCK), F32),
            pltpu.VMEM((GROUP, BLOCK, BLOCK), F32),
            pltpu.VMEM((GROUP, BLOCK, BLOCK), BF16),
            pltpu.VMEM((GROUP, BLOCK, BLOCK), BF16),
            pltpu.VMEM((GROUP, PAD, BLOCK), BF16),
            pltpu.VMEM((GROUP, PAD, BLOCK), BF16),
            pltpu.VMEM((HEADS // 2, HEAD, ROWS), BF16),
            pltpu.SemaphoreType.DMA,
        ],
        compiler_params=pltpu.CompilerParams(vmem_limit_bytes=VMEM_MORE),
        cost_estimate=pl.CostEstimate(flops=10**10, bytes_accessed=0, transcendentals=0),
        name="attend",
    )(me, extents, received)


def unpack_body(y_ref, dq_ref, dk_ref, dv_ref):
    for j, ref in enumerate((dq_ref, dk_ref, dv_ref)):
        rows = [y_ref[h].astype(F32)[j * HEAD : (j + 1) * HEAD] for h in range(HEADS)]
        ref[...] = jnp.concatenate(rows, axis=0).T.astype(BF16)


def unpack(returned):
    shape = jax.ShapeDtypeStruct((ROWS, HEADS * HEAD), BF16)
    return pl.pallas_call(
        unpack_body,
        out_shape=(shape, shape, shape),
        compiler_params=pltpu.CompilerParams(vmem_limit_bytes=VMEM_SOME),
        cost_estimate=pl.CostEstimate(flops=10**11, bytes_accessed=0, transcendentals=0),
        name="unpack",
    )(returned)


def weight_body(tile_ref, mine_ref, got_ref, *refs):
    grads, out_ref = refs[:8], refs[8]
    total = jnp.zeros((2 * HEAD, HEADS * HEAD), F32)
    for i in range(0, 8, 2):
        left = [jnp.concatenate([mine_ref[j], got_ref[j]], axis=0) for j in (i, i + 1)]
        right = jnp.concatenate([grads[i][...], grads[i + 1][...]], axis=0)
        total = total + dot(jnp.concatenate(left, axis=1), right, NN)
    empty = jnp.zeros((STRIP, ROWS - 3 * REST), F32)
    for tile in range(8):
        for head in range(2):
            part = total[head * HEAD : (head + 1) * HEAD, tile * TILE : (tile + 1) * TILE]
            rest = [part[i * STRIP : (i + 1) * STRIP, ROWS:] for i in range(3)]
            rest = jnp.concatenate(rest + [empty], axis=1)
            out_ref[tile_ref[tile], head] = jnp.concatenate([part[:, :ROWS], rest], axis=0).astype(BF16)


def weight_terms(places, mine, got, grads):
    return pl.pallas_call(
        weight_body,
        out_shape=jax.ShapeDtypeStruct((8, 2, HEAD + STRIP, ROWS), BF16),
        in_specs=[pl.BlockSpec(memory_space=pltpu.SMEM)]
        + [pl.BlockSpec(memory_space=pltpu.VMEM)] * 10,
        out_specs=pl.BlockSpec(memory_space=pltpu.VMEM),
        compiler_params=pltpu.CompilerParams(vmem_limit_bytes=VMEM_SOME),
        cost_estimate=pl.CostEstimate(flops=10**9, bytes_accessed=0, transcendentals=0),
        name="weight_terms",
    )(places, mine, got, *grads)


def finish_body(own_ref, *refs):
    total = own_ref[...]
    for ref in refs[:-1]:
        total = total + ref[...].astype(F32)
    rest = [total[HEAD:, i * REST : (i + 1) * REST] for i in range(3)]
    refs[-1][...] = jnp.concatenate([total[:HEAD], jnp.concatenate(rest, axis=0)], axis=1)


def finish(own, others):
    return pl.pallas_call(
        finish_body,
        out_shape=jax.ShapeDtypeStruct((HEAD, TILE), F32),
        compiler_params=pltpu.CompilerParams(vmem_limit_bytes=VMEM_SOME),
        name="finish",
    )(own, *others)


def swap(x, axis, size, apart):
    return lax.ppermute(x, axis, [(i, i ^ apart) for i in range(size)])


def local(queries, keys, values, out_grad, out_weight, extents):
    me = lax.axis_index("seq")
    part = lax.axis_index("dp")

    sent = pack(queries, keys, values, out_grad, out_weight)
    received = lax.all_to_all(sent, "seq", 0, 0, tiled=True)
    late, received = lax.optimization_barrier((out_grad, received))
    far = [out_grad] + [swap(late, "seq", HEADS, apart) for apart in (2, 8, 10)]
    grads, mine, give = attend(me[None].astype(jnp.int32), extents, received)
    got = swap(give, "seq", HEADS, 4)
    _, *far = lax.optimization_barrier((give, *far))
    near = [swap(x, "seq", HEADS, 1) for x in far]
    out_grads = [x for pair in zip(far, near) for x in pair]
    returned = lax.all_to_all(grads, "seq", 0, 0, tiled=True)

    x_lo, y = part // 4, part % 4
    tile = jnp.arange(8, dtype=jnp.int32)
    places = ((tile // 4) ^ x_lo) + 2 * ((tile % 4) ^ y)
    terms = weight_terms(places.astype(jnp.int32), mine, got, out_grads)
    total = terms[:2].astype(F32)
    for apart in (1, 2, 3):
        total = total + swap(terms[2 * apart : 2 * apart + 2], "dp", 8, apart).astype(F32)
    last = []
    for x_apart, z_apart in ((1, 0), (0, 1), (1, 1)):
        pairs = [(i, i ^ (64 * x_apart + 4 * z_apart)) for i in range(128)]
        last.append(lax.ppermute(total[x_apart, z_apart].astype(BF16), ("dp", "seq"), pairs))
    query_grad, key_grad, value_grad = unpack(returned)
    value_grad, *last = lax.optimization_barrier((value_grad, *last))
    weight_grad = finish(total[0, 0], last)
    return query_grad, key_grad, value_grad, weight_grad


def solution(mesh):
    tokens = P(("dp", "seq"), None)
    return jax.shard_map(
        local,
        mesh=mesh,
        in_specs=(tokens, tokens, tokens, tokens, P(), P("dp", None)),
        out_specs=(tokens, tokens, tokens, P("seq", "dp")),
        check_vma=False,
    )
```

```python
import functools

import jax
import jax.numpy as jnp
from jax import lax
from jax.experimental import pallas as pl
from jax.experimental.pallas import tpu as pltpu
from jax.sharding import PartitionSpec as P

HEADS = 16
HEAD = 72
IMAGES = 8
UNIT = 64
ROWS = 128
BLOCK = 256
BLOCKS = 8
GROUP = 4
PAIRS = BLOCKS * BLOCKS + 3 * GROUP
TILE = 144
REST = TILE - ROWS
STRIP = 24
PARTS = 4
PAD = 80
SCALE = HEAD**-0.5
LOG2E = 1.4426950408889634
FAR = 16384.0
F32 = jnp.float32
BF16 = jnp.bfloat16
VMEM_SOME = 12 << 20
VMEM_MORE = 36 << 20
VMEM_MOST = (64 << 20) - (128 << 10)

NN = (((1,), (0,)), ((), ()))
NT = (((1,), (1,)), ((), ()))


def dot(a, b, dims):
    return lax.dot_general(a, b, dims, preferred_element_type=F32)


def pack_body(
    q_hbm, k_hbm, v_hbm, g_hbm, w_hbm, out_hbm, q_ref, k_ref, v_ref, g_ref, w_ref, out_ref, sems, out_sems
):
    width = HEADS * HEAD // PARTS
    heads = HEADS // PARTS
    ins = [
        pltpu.make_async_copy(source, target, sems.at[i])
        for i, (source, target) in enumerate(
            [(q_hbm, q_ref), (k_hbm, k_ref), (v_hbm, v_ref), (g_hbm, g_ref)]
            + [(w_hbm.at[pl.ds(p * width, width)], w_ref.at[p]) for p in range(PARTS)]
        )
    ]
    for copy in ins:
        copy.start()
    turned = []
    for i, ref in enumerate((q_ref, k_ref, v_ref)):
        ins[i].wait()
        turned.append(ref[...].astype(F32).T)
    ins[3].wait()
    outs = []
    for p in range(PARTS):
        ins[4 + p].wait()
        back = dot(w_ref[p], g_ref[...], NT).astype(BF16).astype(F32)
        for i in range(heads):
            h = p * heads + i
            rows = [x[h * HEAD : (h + 1) * HEAD] for x in turned]
            rows.append(back[i * HEAD : (i + 1) * HEAD])
            out_ref[h] = jnp.concatenate(rows, axis=0).astype(BF16)
        part = pl.ds(p * heads, heads)
        outs.append(pltpu.make_async_copy(out_ref.at[part], out_hbm.at[part], out_sems.at[p]))
        outs[p].start()
    for copy in outs:
        copy.wait()


def pack(queries, keys, values, out_grad, out_weight):
    width = HEADS * HEAD
    shape = (HEADS, 4 * HEAD, ROWS)
    return pl.pallas_call(
        pack_body,
        out_shape=jax.ShapeDtypeStruct(shape, BF16),
        in_specs=[pl.BlockSpec(memory_space=pltpu.HBM)] * 5,
        out_specs=pl.BlockSpec(memory_space=pl.ANY),
        scratch_shapes=[pltpu.VMEM((ROWS, width), BF16)] * 4
        + [
            pltpu.VMEM((PARTS, width // PARTS, width), BF16),
            pltpu.VMEM(shape, BF16),
            pltpu.SemaphoreType.DMA((4 + PARTS,)),
            pltpu.SemaphoreType.DMA((PARTS,)),
        ],
        compiler_params=pltpu.CompilerParams(vmem_limit_bytes=VMEM_MOST),
        cost_estimate=pl.CostEstimate(flops=10**10, bytes_accessed=0, transcendentals=0),
        name="pack",
    )(queries, keys, values, out_grad, out_weight)


def kept(total, later):
    return jnp.where(later > 0, total, 0.0)


def attend_body(
    me_ref, ext_ref, r_ref, g_ref, mine_hbm, give_ref, q_s, b_s, k_s, v_s, kn_s, vn_s, e_s, acc_s, dq_s, dk_s, dv_s,
    top_s, pair_top_s, delta_s, inverse_s, qb_s, kb_s, later_q_s, later_k_s,
    even_s, odd_s, ds_even_s, ds_odd_s, back_even_s, back_odd_s, mine_ref, mine_sem
):
    ends = []
    total = jnp.int32(0)
    for i in range(IMAGES):
        total = total + ext_ref[0, i] * UNIT
        ends.append(total)

    lane = lax.broadcasted_iota(jnp.int32, (IMAGES, ROWS), 1)
    row = lax.broadcasted_iota(jnp.int32, (IMAGES, ROWS), 0)
    nothing = jnp.zeros((128 - PAD, ROWS), F32)
    ones_row = jnp.where(row == 0, 1.0, 0.0)
    zeros_rows = jnp.zeros((IMAGES, ROWS), F32)
    for s in range(HEADS):
        b, half = s // 2, s % 2
        lanes = slice(half * ROWS, (half + 1) * ROWS)
        x = r_ref[s].astype(F32)
        q, k, v, back = (x[j * HEAD : (j + 1) * HEAD] for j in range(4))
        segment = jnp.zeros((IMAGES, ROWS), jnp.int32)
        for end in ends:
            segment = segment + (lane + s * ROWS >= end).astype(jnp.int32)
        here = (segment == row).astype(F32)
        q_s[b, :, lanes] = jnp.concatenate([q, here * -FAR, nothing], axis=0).astype(BF16)
        b_s[b, :, lanes] = jnp.concatenate([back, zeros_rows], axis=0).astype(BF16)
        k_aug = jnp.concatenate([k, 1.0 - here, nothing], axis=0)
        v_aug = jnp.concatenate([v, zeros_rows, nothing], axis=0)
        k_s[b, :, lanes] = k_aug[:PAD].astype(BF16)
        v_s[b, :, lanes] = jnp.concatenate([v, ones_row], axis=0).astype(BF16)
        kn_s[b, lanes, :] = k_aug.T.astype(BF16)
        vn_s[b, lanes, :] = v_aug.T.astype(BF16)

    top_s[...] = jnp.full(top_s.shape, -3e38, F32)

    count = jnp.int32(0)
    reached = jnp.int32(0)
    for qb in range(BLOCKS):
        first, last = qb * BLOCK, qb * BLOCK + BLOCK - 1
        start, stop = jnp.int32(0), jnp.int32(BLOCKS * BLOCK)
        for end in ends:
            start = jnp.maximum(start, jnp.where(end <= first, end, 0))
            stop = jnp.minimum(stop, jnp.where(end > last, end, BLOCKS * BLOCK))
        lo = start // BLOCK
        size = (stop + BLOCK - 1) // BLOCK - lo

        def add_pair(i, carry, qb=qb, lo=lo, base=count, reached=reached):
            qb_s[base + i] = qb
            kb_s[base + i] = lo + i
            later_q_s[base + i] = i
            later_k_s[base + i] = (lo + i < reached).astype(jnp.int32)
            return carry

        lax.fori_loop(0, size, add_pair, 0)
        count = count + size
        reached = lo + size
    for u in range(3 * GROUP):
        qb_s[count + u] = BLOCKS
        kb_s[count + u] = BLOCKS
        later_q_s[count + u] = 0
        later_k_s[count + u] = 0

    def score(at, ref, u):
        scores = dot(kn_s[kb_s[at]][:, :PAD], q_s[qb_s[at]][:PAD], NN)
        ref[u] = scores
        top = jnp.max(scores.reshape(BLOCK // 8, 8, BLOCK), axis=0)
        pair_top_s[at] = jnp.max(top, axis=0, keepdims=True)

    def soften(at, ref, u):
        e = jnp.exp2((ref[u] - pair_top_s[at]) * (SCALE * LOG2E))
        e_s[at] = e
        return dot(v_s[kb_s[at]], e.astype(BF16), NN)

    def gather(at, term):
        qb, top = qb_s[at], pair_top_s[at]
        before = top_s[qb]
        after = jnp.maximum(before, top)
        top_s[qb] = after
        acc_s[qb] = kept(acc_s[qb], later_q_s[at]) * jnp.exp2(
            (before - after) * (SCALE * LOG2E)
        ) + term * jnp.exp2((top - after) * (SCALE * LOG2E))

    def forward(i, carry):
        for first, now, ahead in ((2 * i, even_s, odd_s), (2 * i + 1, odd_s, even_s)):
            terms = []
            for u in range(GROUP):
                score((first + 1) * GROUP + u, ahead, u)
                terms.append(soften(first * GROUP + u, now, u))
            for u in range(GROUP):
                gather(first * GROUP + u, terms[u])
        return carry

    rounds = (count + 2 * GROUP - 1) // (2 * GROUP)
    for u in range(GROUP):
        score(u, even_s, u)
    lax.fori_loop(0, rounds, forward, 0)

    for qb in range(BLOCKS):
        acc = acc_s[qb]
        inverse = 1.0 / acc[HEAD : HEAD + 1]
        attended = (acc[:HEAD] * inverse).astype(BF16)
        for half in range(2):
            apart = (2 * qb + half) ^ me_ref[0]
            place = (apart & 3) + ((apart >> 3) << 2)
            rows = attended[:, half * ROWS : (half + 1) * ROWS]

            @pl.when(apart & 4 == 0)
            def _(place=place, rows=rows):
                mine_ref[place] = rows

            @pl.when(apart & 4 != 0)
            def _(place=place, rows=rows):
                give_ref[place] = rows

        back = b_s[qb].astype(F32)
        delta_s[qb] = jnp.sum(back[:HEAD] * attended.astype(F32), axis=0, keepdims=True)
        inverse_s[qb] = inverse

    keep = pltpu.make_async_copy(mine_ref, mine_hbm, mine_sem)
    keep.start()

    def differ(at, ds_ref, back_ref, u):
        qb = qb_s[at]
        factor = jnp.exp2((pair_top_s[at] - top_s[qb]) * (SCALE * LOG2E)) * inverse_s[qb]
        back = (b_s[qb].astype(F32) * factor).astype(BF16)
        back_ref[u] = back
        dprobs = dot(vn_s[kb_s[at]][:, :PAD], back, NN)
        ds_ref[u] = (e_s[at] * (dprobs - delta_s[qb] * factor)).astype(BF16)

    def products(at, ds_ref, back_ref, u):
        dv = dot(back_ref[u], e_s[at].astype(BF16), NT)
        dk = dot(q_s[qb_s[at]][:PAD], ds_ref[u], NT)
        dq = dot(k_s[kb_s[at]], ds_ref[u], NN)
        return dv, dk, dq

    def collect(at, dv, dk, dq):
        qb, kb = qb_s[at], kb_s[at]
        dv_s[kb] = kept(dv_s[kb], later_k_s[at]) + dv
        dk_s[kb] = kept(dk_s[kb], later_k_s[at]) + dk
        dq_s[qb] = kept(dq_s[qb], later_q_s[at]) + dq

    def backward(i, carry):
        for first, now, ahead in ((2 * i, even, odd), (2 * i + 1, odd, even)):
            terms = []
            for u in range(GROUP):
                differ((first + 1) * GROUP + u, *ahead, u)
                terms.append(products(first * GROUP + u, *now, u))
            for u in range(GROUP):
                collect(first * GROUP + u, *terms[u])
        return carry

    even, odd = (ds_even_s, back_even_s), (ds_odd_s, back_odd_s)
    for u in range(GROUP):
        differ(u, *even, u)
    lax.fori_loop(0, rounds, backward, 0)

    for s in range(HEADS):
        b, half = s // 2, s % 2
        lanes = slice(half * ROWS, (half + 1) * ROWS)
        g_ref[s] = jnp.concatenate(
            [
                dq_s[b, :HEAD, lanes] * SCALE,
                dk_s[b, :HEAD, lanes] * SCALE,
                dv_s[b, :HEAD, lanes],
            ],
            axis=0,
        ).astype(BF16)
    keep.wait()


def attend(me, extents, received):
    return pl.pallas_call(
        attend_body,
        out_shape=(
            jax.ShapeDtypeStruct((HEADS, 3 * HEAD, ROWS), BF16),
            jax.ShapeDtypeStruct((HEADS // 2, HEAD, ROWS), BF16),
            jax.ShapeDtypeStruct((HEADS // 2, HEAD, ROWS), BF16),
        ),
        in_specs=[
            pl.BlockSpec(memory_space=pltpu.SMEM),
            pl.BlockSpec(memory_space=pltpu.SMEM),
            pl.BlockSpec(memory_space=pltpu.VMEM),
        ],
        out_specs=(
            pl.BlockSpec(memory_space=pltpu.VMEM),
            pl.BlockSpec(memory_space=pltpu.HBM),
            pl.BlockSpec(memory_space=pltpu.VMEM),
        ),
        scratch_shapes=[
            pltpu.VMEM((BLOCKS + 1, 128, BLOCK), BF16),
            pltpu.VMEM((BLOCKS + 1, PAD, BLOCK), BF16),
            pltpu.VMEM((BLOCKS + 1, PAD, BLOCK), BF16),
            pltpu.VMEM((BLOCKS + 1, PAD, BLOCK), BF16),
            pltpu.VMEM((BLOCKS + 1, BLOCK, 128), BF16),
            pltpu.VMEM((BLOCKS + 1, BLOCK, 128), BF16),
            pltpu.VMEM((PAIRS, BLOCK, BLOCK), F32),
            pltpu.VMEM((BLOCKS + 1, PAD, BLOCK), F32),
            pltpu.VMEM((BLOCKS + 1, PAD, BLOCK), F32),
            pltpu.VMEM((BLOCKS + 1, PAD, BLOCK), F32),
            pltpu.VMEM((BLOCKS + 1, PAD, BLOCK), F32),
            pltpu.VMEM((BLOCKS + 1, 1, BLOCK), F32),
            pltpu.VMEM((PAIRS, 1, BLOCK), F32),
            pltpu.VMEM((BLOCKS + 1, 1, BLOCK), F32),
            pltpu.VMEM((BLOCKS + 1, 1, BLOCK), F32),
            pltpu.SMEM((PAIRS,), jnp.int32),
            pltpu.SMEM((PAIRS,), jnp.int32),
            pltpu.SMEM((PAIRS,), jnp.int32),
            pltpu.SMEM((PAIRS,), jnp.int32),
            pltpu.VMEM((GROUP, BLOCK, BLOCK), F32),
            pltpu.VMEM((GROUP, BLOCK, BLOCK), F32),
            pltpu.VMEM((GROUP, BLOCK, BLOCK), BF16),
            pltpu.VMEM((GROUP, BLOCK, BLOCK), BF16),
            pltpu.VMEM((GROUP, PAD, BLOCK), BF16),
            pltpu.VMEM((GROUP, PAD, BLOCK), BF16),
            pltpu.VMEM((HEADS // 2, HEAD, ROWS), BF16),
            pltpu.SemaphoreType.DMA,
        ],
        compiler_params=pltpu.CompilerParams(vmem_limit_bytes=VMEM_MORE),
        cost_estimate=pl.CostEstimate(flops=10**10, bytes_accessed=0, transcendentals=0),
        name="attend",
    )(me, extents, received)


def unpack_body(y_ref, dq_ref, dk_ref, dv_ref):
    for j, ref in enumerate((dq_ref, dk_ref, dv_ref)):
        rows = [y_ref[h].astype(F32)[j * HEAD : (j + 1) * HEAD] for h in range(HEADS)]
        ref[...] = jnp.concatenate(rows, axis=0).T.astype(BF16)


def unpack(returned):
    shape = jax.ShapeDtypeStruct((ROWS, HEADS * HEAD), BF16)
    return pl.pallas_call(
        unpack_body,
        out_shape=(shape, shape, shape),
        compiler_params=pltpu.CompilerParams(vmem_limit_bytes=VMEM_SOME),
        cost_estimate=pl.CostEstimate(flops=10**11, bytes_accessed=0, transcendentals=0),
        name="unpack",
    )(returned)


def weight_body(tile_ref, mine_ref, got_ref, *refs):
    grads, out_ref = refs[:8], refs[8]
    total = jnp.zeros((2 * HEAD, HEADS * HEAD), F32)
    for i in range(0, 8, 2):
        left = [jnp.concatenate([mine_ref[j], got_ref[j]], axis=0) for j in (i, i + 1)]
        right = jnp.concatenate([grads[i][...], grads[i + 1][...]], axis=0)
        total = total + dot(jnp.concatenate(left, axis=1), right, NN)
    empty = jnp.zeros((STRIP, ROWS - 3 * REST), F32)
    for tile in range(8):
        for head in range(2):
            part = total[head * HEAD : (head + 1) * HEAD, tile * TILE : (tile + 1) * TILE]
            rest = [part[i * STRIP : (i + 1) * STRIP, ROWS:] for i in range(3)]
            rest = jnp.concatenate(rest + [empty], axis=1)
            out_ref[tile_ref[tile], head] = jnp.concatenate([part[:, :ROWS], rest], axis=0).astype(BF16)


def weight_terms(places, mine, got, grads):
    return pl.pallas_call(
        weight_body,
        out_shape=jax.ShapeDtypeStruct((8, 2, HEAD + STRIP, ROWS), BF16),
        in_specs=[pl.BlockSpec(memory_space=pltpu.SMEM)]
        + [pl.BlockSpec(memory_space=pltpu.VMEM)] * 10,
        out_specs=pl.BlockSpec(memory_space=pltpu.VMEM),
        compiler_params=pltpu.CompilerParams(vmem_limit_bytes=VMEM_SOME),
        cost_estimate=pl.CostEstimate(flops=10**9, bytes_accessed=0, transcendentals=0),
        name="weight_terms",
    )(places, mine, got, *grads)


def finish_body(own_ref, *refs):
    total = own_ref[...]
    for ref in refs[:-1]:
        total = total + ref[...].astype(F32)
    rest = [total[HEAD:, i * REST : (i + 1) * REST] for i in range(3)]
    refs[-1][...] = jnp.concatenate([total[:HEAD], jnp.concatenate(rest, axis=0)], axis=1)


def finish(own, others):
    return pl.pallas_call(
        finish_body,
        out_shape=jax.ShapeDtypeStruct((HEAD, TILE), F32),
        compiler_params=pltpu.CompilerParams(vmem_limit_bytes=VMEM_SOME),
        name="finish",
    )(own, *others)


def swap(x, axis, size, apart):
    return lax.ppermute(x, axis, [(i, i ^ apart) for i in range(size)])


def local(queries, keys, values, out_grad, out_weight, extents):
    me = lax.axis_index("seq")
    part = lax.axis_index("dp")

    sent = pack(queries, keys, values, out_grad, out_weight)
    received = lax.all_to_all(sent, "seq", 0, 0, tiled=True)
    late, received = lax.optimization_barrier((out_grad, received))
    far = [out_grad] + [swap(late, "seq", HEADS, apart) for apart in (2, 8, 10)]
    grads, mine, give = attend(me[None].astype(jnp.int32), extents, received)
    got = swap(give, "seq", HEADS, 4)
    near = [swap(out_grad, "seq", HEADS, 1)]
    _, *far[1:] = lax.optimization_barrier((got, *far[1:]))
    for x in far[1:]:
        halves = [swap(x[i : i + 64], "seq", HEADS, 1) for i in (0, 64)]
        near.append(jnp.concatenate(halves, axis=0))
    out_grads = [x for pair in zip(far, near) for x in pair]
    returned = lax.all_to_all(grads, "seq", 0, 0, tiled=True)

    x_lo, y = part // 4, part % 4
    tile = jnp.arange(8, dtype=jnp.int32)
    places = ((tile // 4) ^ x_lo) + 2 * ((tile % 4) ^ y)
    terms = weight_terms(places.astype(jnp.int32), mine, got, out_grads)
    total = terms[:2].astype(F32)
    for apart in (1, 2, 3):
        total = total + swap(terms[2 * apart : 2 * apart + 2], "dp", 8, apart).astype(F32)
    last = []
    for x_apart, z_apart in ((1, 0), (0, 1), (1, 1)):
        pairs = [(i, i ^ (64 * x_apart + 4 * z_apart)) for i in range(128)]
        last.append(lax.ppermute(total[x_apart, z_apart].astype(BF16), ("dp", "seq"), pairs))
    query_grad, key_grad, value_grad = unpack(returned)
    value_grad, *last = lax.optimization_barrier((value_grad, *last))
    weight_grad = finish(total[0, 0], last)
    return query_grad, key_grad, value_grad, weight_grad


def solution(mesh):
    tokens = P(("dp", "seq"), None)
    return jax.shard_map(
        local,
        mesh=mesh,
        in_specs=(tokens, tokens, tokens, tokens, P(), P("dp", None)),
        out_specs=(tokens, tokens, tokens, P("seq", "dp")),
        check_vma=False,
    )
```

```python
import functools

import jax
import jax.numpy as jnp
from jax import lax
from jax.experimental import pallas as pl
from jax.experimental.pallas import tpu as pltpu
from jax.sharding import PartitionSpec as P

HEADS = 16
HEAD = 72
IMAGES = 8
UNIT = 64
ROWS = 128
BLOCK = 256
BLOCKS = 8
GROUP = 8
PAIRS = BLOCKS * BLOCKS + 3 * GROUP
TILE = 144
REST = TILE - ROWS
STRIP = 24
PARTS = 4
PAD = 80
SCALE = HEAD**-0.5
LOG2E = 1.4426950408889634
FAR = 16384.0
F32 = jnp.float32
BF16 = jnp.bfloat16
VMEM_SOME = 12 << 20
VMEM_MORE = 40 << 20
VMEM_MOST = (64 << 20) - (128 << 10)

NN = (((1,), (0,)), ((), ()))
NT = (((1,), (1,)), ((), ()))


def dot(a, b, dims):
    return lax.dot_general(a, b, dims, preferred_element_type=F32)


def pack_body(
    q_hbm, k_hbm, v_hbm, g_hbm, w_hbm, out_hbm, q_ref, k_ref, v_ref, g_ref, w_ref, out_ref, sems, out_sems
):
    width = HEADS * HEAD // PARTS
    heads = HEADS // PARTS
    ins = [
        pltpu.make_async_copy(source, target, sems.at[i])
        for i, (source, target) in enumerate(
            [(q_hbm, q_ref), (k_hbm, k_ref), (v_hbm, v_ref), (g_hbm, g_ref)]
            + [(w_hbm.at[pl.ds(p * width, width)], w_ref.at[p]) for p in range(PARTS)]
        )
    ]
    for copy in ins:
        copy.start()
    turned = []
    for i, ref in enumerate((q_ref, k_ref, v_ref)):
        ins[i].wait()
        turned.append(ref[...].astype(F32).T)
    ins[3].wait()
    outs = []
    for p in range(PARTS):
        ins[4 + p].wait()
        back = dot(w_ref[p], g_ref[...], NT).astype(BF16).astype(F32)
        for i in range(heads):
            h = p * heads + i
            rows = [x[h * HEAD : (h + 1) * HEAD] for x in turned]
            rows.append(back[i * HEAD : (i + 1) * HEAD])
            out_ref[h] = jnp.concatenate(rows, axis=0).astype(BF16)
        part = pl.ds(p * heads, heads)
        outs.append(pltpu.make_async_copy(out_ref.at[part], out_hbm.at[part], out_sems.at[p]))
        outs[p].start()
    for copy in outs:
        copy.wait()


def pack(queries, keys, values, out_grad, out_weight):
    width = HEADS * HEAD
    shape = (HEADS, 4 * HEAD, ROWS)
    return pl.pallas_call(
        pack_body,
        out_shape=jax.ShapeDtypeStruct(shape, BF16),
        in_specs=[pl.BlockSpec(memory_space=pltpu.HBM)] * 5,
        out_specs=pl.BlockSpec(memory_space=pl.ANY),
        scratch_shapes=[pltpu.VMEM((ROWS, width), BF16)] * 4
        + [
            pltpu.VMEM((PARTS, width // PARTS, width), BF16),
            pltpu.VMEM(shape, BF16),
            pltpu.SemaphoreType.DMA((4 + PARTS,)),
            pltpu.SemaphoreType.DMA((PARTS,)),
        ],
        compiler_params=pltpu.CompilerParams(vmem_limit_bytes=VMEM_MOST),
        cost_estimate=pl.CostEstimate(flops=10**10, bytes_accessed=0, transcendentals=0),
        name="pack",
    )(queries, keys, values, out_grad, out_weight)


def kept(total, later):
    return jnp.where(later > 0, total, 0.0)


def attend_body(
    me_ref, ext_ref, r_ref, g_ref, mine_hbm, give_ref, q_s, b_s, k_s, v_s, kn_s, vn_s, e_s, acc_s, dq_s, dk_s, dv_s,
    top_s, pair_top_s, delta_s, inverse_s, qb_s, kb_s, later_q_s, later_k_s,
    even_s, odd_s, ds_even_s, ds_odd_s, back_even_s, back_odd_s, mine_ref, mine_sem
):
    ends = []
    total = jnp.int32(0)
    for i in range(IMAGES):
        total = total + ext_ref[0, i] * UNIT
        ends.append(total)

    lane = lax.broadcasted_iota(jnp.int32, (IMAGES, ROWS), 1)
    row = lax.broadcasted_iota(jnp.int32, (IMAGES, ROWS), 0)
    nothing = jnp.zeros((128 - PAD, ROWS), F32)
    ones_row = jnp.where(row == 0, 1.0, 0.0)
    zeros_rows = jnp.zeros((IMAGES, ROWS), F32)
    for s in range(HEADS):
        b, half = s // 2, s % 2
        lanes = slice(half * ROWS, (half + 1) * ROWS)
        x = r_ref[s].astype(F32)
        q, k, v, back = (x[j * HEAD : (j + 1) * HEAD] for j in range(4))
        segment = jnp.zeros((IMAGES, ROWS), jnp.int32)
        for end in ends:
            segment = segment + (lane + s * ROWS >= end).astype(jnp.int32)
        here = (segment == row).astype(F32)
        q_s[b, :, lanes] = jnp.concatenate([q, here * -FAR, nothing], axis=0).astype(BF16)
        b_s[b, :, lanes] = jnp.concatenate([back, zeros_rows], axis=0).astype(BF16)
        k_aug = jnp.concatenate([k, 1.0 - here, nothing], axis=0)
        v_aug = jnp.concatenate([v, zeros_rows, nothing], axis=0)
        k_s[b, :, lanes] = k_aug[:PAD].astype(BF16)
        v_s[b, :, lanes] = jnp.concatenate([v, ones_row], axis=0).astype(BF16)
        kn_s[b, lanes, :] = k_aug.T.astype(BF16)
        vn_s[b, lanes, :] = v_aug.T.astype(BF16)

    top_s[...] = jnp.full(top_s.shape, -3e38, F32)

    count = jnp.int32(0)
    reached = jnp.int32(0)
    for qb in range(BLOCKS):
        first, last = qb * BLOCK, qb * BLOCK + BLOCK - 1
        start, stop = jnp.int32(0), jnp.int32(BLOCKS * BLOCK)
        for end in ends:
            start = jnp.maximum(start, jnp.where(end <= first, end, 0))
            stop = jnp.minimum(stop, jnp.where(end > last, end, BLOCKS * BLOCK))
        lo = start // BLOCK
        size = (stop + BLOCK - 1) // BLOCK - lo

        def add_pair(i, carry, qb=qb, lo=lo, base=count, reached=reached):
            qb_s[base + i] = qb
            kb_s[base + i] = lo + i
            later_q_s[base + i] = i
            later_k_s[base + i] = (lo + i < reached).astype(jnp.int32)
            return carry

        lax.fori_loop(0, size, add_pair, 0)
        count = count + size
        reached = lo + size
    for u in range(3 * GROUP):
        qb_s[count + u] = BLOCKS
        kb_s[count + u] = BLOCKS
        later_q_s[count + u] = 0
        later_k_s[count + u] = 0

    def score(at, ref, u):
        scores = dot(kn_s[kb_s[at]][:, :PAD], q_s[qb_s[at]][:PAD], NN)
        ref[u] = scores
        top = jnp.max(scores.reshape(BLOCK // 8, 8, BLOCK), axis=0)
        pair_top_s[at] = jnp.max(top, axis=0, keepdims=True)

    def soften(at, ref, u):
        e = jnp.exp2((ref[u] - pair_top_s[at]) * (SCALE * LOG2E))
        e_s[at] = e
        return dot(v_s[kb_s[at]], e.astype(BF16), NN)

    def gather(at, term):
        qb, top = qb_s[at], pair_top_s[at]
        before = top_s[qb]
        after = jnp.maximum(before, top)
        top_s[qb] = after
        acc_s[qb] = kept(acc_s[qb], later_q_s[at]) * jnp.exp2(
            (before - after) * (SCALE * LOG2E)
        ) + term * jnp.exp2((top - after) * (SCALE * LOG2E))

    def forward(i, carry):
        for first, now, ahead in ((2 * i, even_s, odd_s), (2 * i + 1, odd_s, even_s)):
            terms = []
            for u in range(GROUP):
                score((first + 1) * GROUP + u, ahead, u)
                terms.append(soften(first * GROUP + u, now, u))
            for u in range(GROUP):
                gather(first * GROUP + u, terms[u])
        return carry

    rounds = (count + 2 * GROUP - 1) // (2 * GROUP)
    for u in range(GROUP):
        score(u, even_s, u)
    lax.fori_loop(0, rounds, forward, 0)

    for qb in range(BLOCKS):
        acc = acc_s[qb]
        inverse = 1.0 / acc[HEAD : HEAD + 1]
        attended = (acc[:HEAD] * inverse).astype(BF16)
        for half in range(2):
            apart = (2 * qb + half) ^ me_ref[0]
            place = (apart & 3) + ((apart >> 3) << 2)
            rows = attended[:, half * ROWS : (half + 1) * ROWS]

            @pl.when(apart & 4 == 0)
            def _(place=place, rows=rows):
                mine_ref[place] = rows

            @pl.when(apart & 4 != 0)
            def _(place=place, rows=rows):
                give_ref[place] = rows

        back = b_s[qb].astype(F32)
        delta_s[qb] = jnp.sum(back[:HEAD] * attended.astype(F32), axis=0, keepdims=True)
        inverse_s[qb] = inverse

    keep = pltpu.make_async_copy(mine_ref, mine_hbm, mine_sem)
    keep.start()

    def differ(at, ds_ref, back_ref, u):
        qb = qb_s[at]
        factor = jnp.exp2((pair_top_s[at] - top_s[qb]) * (SCALE * LOG2E)) * inverse_s[qb]
        back = (b_s[qb].astype(F32) * factor).astype(BF16)
        back_ref[u] = back
        dprobs = dot(vn_s[kb_s[at]][:, :PAD], back, NN)
        ds_ref[u] = (e_s[at] * (dprobs - delta_s[qb] * factor)).astype(BF16)

    def products(at, ds_ref, back_ref, u):
        dv = dot(back_ref[u], e_s[at].astype(BF16), NT)
        dk = dot(q_s[qb_s[at]][:PAD], ds_ref[u], NT)
        dq = dot(k_s[kb_s[at]], ds_ref[u], NN)
        return dv, dk, dq

    def collect(at, dv, dk, dq):
        qb, kb = qb_s[at], kb_s[at]
        dv_s[kb] = kept(dv_s[kb], later_k_s[at]) + dv
        dk_s[kb] = kept(dk_s[kb], later_k_s[at]) + dk
        dq_s[qb] = kept(dq_s[qb], later_q_s[at]) + dq

    def backward(i, carry):
        for first, now, ahead in ((2 * i, even, odd), (2 * i + 1, odd, even)):
            terms = []
            for u in range(GROUP):
                differ((first + 1) * GROUP + u, *ahead, u)
                terms.append(products(first * GROUP + u, *now, u))
            for u in range(GROUP):
                collect(first * GROUP + u, *terms[u])
        return carry

    even, odd = (ds_even_s, back_even_s), (ds_odd_s, back_odd_s)
    for u in range(GROUP):
        differ(u, *even, u)
    lax.fori_loop(0, rounds, backward, 0)

    for s in range(HEADS):
        b, half = s // 2, s % 2
        lanes = slice(half * ROWS, (half + 1) * ROWS)
        g_ref[s] = jnp.concatenate(
            [
                dq_s[b, :HEAD, lanes] * SCALE,
                dk_s[b, :HEAD, lanes] * SCALE,
                dv_s[b, :HEAD, lanes],
            ],
            axis=0,
        ).astype(BF16)
    keep.wait()


def attend(me, extents, received):
    return pl.pallas_call(
        attend_body,
        out_shape=(
            jax.ShapeDtypeStruct((HEADS, 3 * HEAD, ROWS), BF16),
            jax.ShapeDtypeStruct((HEADS // 2, HEAD, ROWS), BF16),
            jax.ShapeDtypeStruct((HEADS // 2, HEAD, ROWS), BF16),
        ),
        in_specs=[
            pl.BlockSpec(memory_space=pltpu.SMEM),
            pl.BlockSpec(memory_space=pltpu.SMEM),
            pl.BlockSpec(memory_space=pltpu.VMEM),
        ],
        out_specs=(
            pl.BlockSpec(memory_space=pltpu.VMEM),
            pl.BlockSpec(memory_space=pltpu.HBM),
            pl.BlockSpec(memory_space=pltpu.VMEM),
        ),
        scratch_shapes=[
            pltpu.VMEM((BLOCKS + 1, 128, BLOCK), BF16),
            pltpu.VMEM((BLOCKS + 1, PAD, BLOCK), BF16),
            pltpu.VMEM((BLOCKS + 1, PAD, BLOCK), BF16),
            pltpu.VMEM((BLOCKS + 1, PAD, BLOCK), BF16),
            pltpu.VMEM((BLOCKS + 1, BLOCK, 128), BF16),
            pltpu.VMEM((BLOCKS + 1, BLOCK, 128), BF16),
            pltpu.VMEM((PAIRS, BLOCK, BLOCK), F32),
            pltpu.VMEM((BLOCKS + 1, PAD, BLOCK), F32),
            pltpu.VMEM((BLOCKS + 1, PAD, BLOCK), F32),
            pltpu.VMEM((BLOCKS + 1, PAD, BLOCK), F32),
            pltpu.VMEM((BLOCKS + 1, PAD, BLOCK), F32),
            pltpu.VMEM((BLOCKS + 1, 1, BLOCK), F32),
            pltpu.VMEM((PAIRS, 1, BLOCK), F32),
            pltpu.VMEM((BLOCKS + 1, 1, BLOCK), F32),
            pltpu.VMEM((BLOCKS + 1, 1, BLOCK), F32),
            pltpu.SMEM((PAIRS,), jnp.int32),
            pltpu.SMEM((PAIRS,), jnp.int32),
            pltpu.SMEM((PAIRS,), jnp.int32),
            pltpu.SMEM((PAIRS,), jnp.int32),
            pltpu.VMEM((GROUP, BLOCK, BLOCK), F32),
            pltpu.VMEM((GROUP, BLOCK, BLOCK), F32),
            pltpu.VMEM((GROUP, BLOCK, BLOCK), BF16),
            pltpu.VMEM((GROUP, BLOCK, BLOCK), BF16),
            pltpu.VMEM((GROUP, PAD, BLOCK), BF16),
            pltpu.VMEM((GROUP, PAD, BLOCK), BF16),
            pltpu.VMEM((HEADS // 2, HEAD, ROWS), BF16),
            pltpu.SemaphoreType.DMA,
        ],
        compiler_params=pltpu.CompilerParams(vmem_limit_bytes=VMEM_MORE),
        cost_estimate=pl.CostEstimate(flops=10**10, bytes_accessed=0, transcendentals=0),
        name="attend",
    )(me, extents, received)


def unpack_body(y_ref, dq_ref, dk_ref, dv_ref):
    for j, ref in enumerate((dq_ref, dk_ref, dv_ref)):
        rows = [y_ref[h].astype(F32)[j * HEAD : (j + 1) * HEAD] for h in range(HEADS)]
        ref[...] = jnp.concatenate(rows, axis=0).T.astype(BF16)


def unpack(returned):
    shape = jax.ShapeDtypeStruct((ROWS, HEADS * HEAD), BF16)
    return pl.pallas_call(
        unpack_body,
        out_shape=(shape, shape, shape),
        compiler_params=pltpu.CompilerParams(vmem_limit_bytes=VMEM_SOME),
        cost_estimate=pl.CostEstimate(flops=10**11, bytes_accessed=0, transcendentals=0),
        name="unpack",
    )(returned)


def weight_body(tile_ref, mine_ref, got_ref, *refs):
    grads, out_ref = refs[:8], refs[8]
    total = jnp.zeros((2 * HEAD, HEADS * HEAD), F32)
    for i in range(0, 8, 2):
        left = [jnp.concatenate([mine_ref[j], got_ref[j]], axis=0) for j in (i, i + 1)]
        right = jnp.concatenate([grads[i][...], grads[i + 1][...]], axis=0)
        total = total + dot(jnp.concatenate(left, axis=1), right, NN)
    empty = jnp.zeros((STRIP, ROWS - 3 * REST), F32)
    for tile in range(8):
        for head in range(2):
            part = total[head * HEAD : (head + 1) * HEAD, tile * TILE : (tile + 1) * TILE]
            rest = [part[i * STRIP : (i + 1) * STRIP, ROWS:] for i in range(3)]
            rest = jnp.concatenate(rest + [empty], axis=1)
            out_ref[tile_ref[tile], head] = jnp.concatenate([part[:, :ROWS], rest], axis=0).astype(BF16)


def weight_terms(places, mine, got, grads):
    return pl.pallas_call(
        weight_body,
        out_shape=jax.ShapeDtypeStruct((8, 2, HEAD + STRIP, ROWS), BF16),
        in_specs=[pl.BlockSpec(memory_space=pltpu.SMEM)]
        + [pl.BlockSpec(memory_space=pltpu.VMEM)] * 10,
        out_specs=pl.BlockSpec(memory_space=pltpu.VMEM),
        compiler_params=pltpu.CompilerParams(vmem_limit_bytes=VMEM_SOME),
        cost_estimate=pl.CostEstimate(flops=10**9, bytes_accessed=0, transcendentals=0),
        name="weight_terms",
    )(places, mine, got, *grads)


def finish_body(own_ref, *refs):
    total = own_ref[...]
    for ref in refs[:-1]:
        total = total + ref[...].astype(F32)
    rest = [total[HEAD:, i * REST : (i + 1) * REST] for i in range(3)]
    refs[-1][...] = jnp.concatenate([total[:HEAD], jnp.concatenate(rest, axis=0)], axis=1)


def finish(own, others):
    return pl.pallas_call(
        finish_body,
        out_shape=jax.ShapeDtypeStruct((HEAD, TILE), F32),
        compiler_params=pltpu.CompilerParams(vmem_limit_bytes=VMEM_SOME),
        name="finish",
    )(own, *others)


def swap(x, axis, size, apart):
    return lax.ppermute(x, axis, [(i, i ^ apart) for i in range(size)])


def local(queries, keys, values, out_grad, out_weight, extents):
    me = lax.axis_index("seq")
    part = lax.axis_index("dp")

    sent = pack(queries, keys, values, out_grad, out_weight)
    received = lax.all_to_all(sent, "seq", 0, 0, tiled=True)
    late, received = lax.optimization_barrier((out_grad, received))
    far = [out_grad] + [swap(late, "seq", HEADS, apart) for apart in (2, 8, 10)]
    grads, mine, give = attend(me[None].astype(jnp.int32), extents, received)
    got = swap(give, "seq", HEADS, 4)
    near = [swap(out_grad, "seq", HEADS, 1)]
    _, *far[1:] = lax.optimization_barrier((got, *far[1:]))
    for x in far[1:]:
        halves = [swap(x[i : i + 64], "seq", HEADS, 1) for i in (0, 64)]
        near.append(jnp.concatenate(halves, axis=0))
    out_grads = [x for pair in zip(far, near) for x in pair]
    returned = lax.all_to_all(grads, "seq", 0, 0, tiled=True)

    x_lo, y = part // 4, part % 4
    tile = jnp.arange(8, dtype=jnp.int32)
    places = ((tile // 4) ^ x_lo) + 2 * ((tile % 4) ^ y)
    terms = weight_terms(places.astype(jnp.int32), mine, got, out_grads)
    total = terms[:2].astype(F32)
    for apart in (1, 2, 3):
        total = total + swap(terms[2 * apart : 2 * apart + 2], "dp", 8, apart).astype(F32)
    last = []
    for x_apart, z_apart in ((1, 0), (0, 1), (1, 1)):
        pairs = [(i, i ^ (64 * x_apart + 4 * z_apart)) for i in range(128)]
        last.append(lax.ppermute(total[x_apart, z_apart].astype(BF16), ("dp", "seq"), pairs))
    query_grad, key_grad, value_grad = unpack(returned)
    value_grad, *last = lax.optimization_barrier((value_grad, *last))
    weight_grad = finish(total[0, 0], last)
    return query_grad, key_grad, value_grad, weight_grad


def solution(mesh):
    tokens = P(("dp", "seq"), None)
    return jax.shard_map(
        local,
        mesh=mesh,
        in_specs=(tokens, tokens, tokens, tokens, P(), P("dp", None)),
        out_specs=(tokens, tokens, tokens, P("seq", "dp")),
        check_vma=False,
    )
```
